512 devices in a mesh: offset: 8 (over y_lo, x), slab: 64 (over y_hi, z, core).
Axes of the slice: x: 4, y: 4 (y_hi: 2, y_lo: 2; y = y_hi * 2 + y_lo), z: 16, core: 2. Of those that a mesh axis runs over, the one named last changes fastest.
Arguments:
- traces: bfloat16 [8, 8192, 256], P('offset', 'slab'), may hold values from -6 to 6
- centre_ids: int32 [8, 8192, 1], P('offset', 'slab'), may hold values from 0 to 63; in each aligned block of 128 rows (0 to 127, 128 to 255, ..., all dimensions but the last counted through in order) at most 6 rows name the same one
- midpoint_bins: int32 [8, 8192], P('offset', 'slab'), may hold values from 0 to 15
- ray_times: float32 [8, 64, 7, 16, 256], P('offset', 'slab'), may hold values from 16 to 240
- ray_amps: float32 [8, 64, 7, 16, 256], P('offset', 'slab'), may hold values from 0.2 to 2
- beam_lateral: float32 [8, 64, 7, 16], P('offset'), may hold values from 0 to 128
- footprint: int32 [64, 7, 2], replicated, may hold values from 0 to 128, as said below
Outputs:
- image: float32 [256, 8192], P('offset', 'slab')
The draws below stay inside these ranges and needn't reach their ends.
Inputs may be any that keep to these rules, and one draw needn't show every extreme that they name: `centre_ids`: within the rows of one device no centre is named by more than 6 rows. footprint[c, w, 0] is below 64 and footprint[c, w, 1] above it; at w = 3, a centre's own slab, they are 0 and 128.
All inputs are finite; a program needn't handle non-finite values.
Results may differ from the reference program's by a relative error of at most 0.0049.
Values may be sent and summed in bfloat16 or wider, within the bound.
No kernel may reach another device: no remote copies, remote signals or barrier semaphores. Data moves between devices by JAX's collectives and lax.ppermute only.
A program may use at most 64 MiB of HBM per device.

```python
import math
import jax
import jax.numpy as jnp
import numpy as np
from jax import lax

NT = 256
NF = 64
KLO = 8
P_SIZE = 16
BINS = 16
CAP = 6
WIN = 7
TRACE_DEV = 128
ZD = 256
XW = 128
CENTRES = 64
TRACES = 8192
OFFSETS = 8


def draw_footprint(key, part):
    key = jax.random.fold_in(key, 11)
    first_key, end_key = jax.random.split(key)
    first_col = jax.random.randint(first_key, (CENTRES, WIN), 0, XW // 2)
    end_col = jax.random.randint(end_key, (CENTRES, WIN), XW // 2 + 1, XW + 1)
    centre_slot = (jnp.arange(WIN) == (WIN - 1) // 2)[None, :]
    first_col = jnp.where(centre_slot, 0, first_col)
    end_col = jnp.where(centre_slot, XW, end_col)
    return jnp.stack([first_col, end_col], axis=-1).astype(jnp.int32)


def place_ends(array, own_key, smallest, largest):
    longest = array.shape.index(max(array.shape))
    spots = []
    for shift in (0, 1):
        where = [jax.random.randint(jax.random.fold_in(own_key, axis), (), 0, length) for axis, length in enumerate(array.shape)]
        where[longest] = (where[longest] + shift) % array.shape[longest]
        spots.append(tuple(where))
    return array.at[spots[0]].set(smallest).at[spots[1]].set(largest)


def level_of(own_key, shape, shards, smallest, high):
    def one(dim, shards_of):
        steps = jax.random.uniform(jax.random.fold_in(jax.random.fold_in(own_key, 6), dim), (shards_of,), jnp.float32, smallest / len(shards), high / len(shards))
        return jnp.repeat(jnp.exp(steps), shape[dim] // shards_of).reshape((-1,) + (1,) * (len(shape) - dim - 1))

    factor_of = one(*shards[0])
    for cut in shards[1:]:
        factor_of = factor_of * one(*cut)
    return factor_of


def shared_out(rng, own, number, rows, count, top, reach, lean):
    sequence = jax.random.permutation(rng, count)
    heavy_load, usual = portions_of(count, rows * top, reach, lean, True), portions_of(count, rows * top, reach, lean, False)
    places = jnp.arange(count)

    def named(lengths, offset_by):
        used = int((lengths > 0).sum())
        fixed = max(1, used // 4)
        passed = fixed + (places - fixed + offset_by * (used - fixed)) % max(1, count - fixed)
        return jnp.zeros((count,), jnp.int32).at[sequence[jnp.where(places < fixed, places, passed)]].set(jnp.asarray(lengths, jnp.int32))

    lengths = jnp.where(number % 4 == 0, named(heavy_load, number // 4), named(usual, number - number // 4 - 1))
    mixed = jax.random.permutation(jax.random.fold_in(own, 3), count)
    giver, receiver = mixed[0:count // 2 * 2:2], mixed[1:count // 2 * 2:2]
    slack = jnp.minimum(lengths[giver] - 1, reach - lengths[receiver]) // 2
    slack = jnp.where((giver == sequence[0]) | (receiver == sequence[0]) | (lengths[receiver] == 0), 0, jnp.maximum(slack, 0))
    passed = jax.random.randint(jax.random.fold_in(own, 4), (count // 2,), 0, 1 << 20) % (slack + 1)
    lengths = lengths.at[giver].add(-passed).at[receiver].add(passed)
    members = jnp.searchsorted(jnp.cumsum(lengths), jnp.arange(rows * top), side="right").astype(jnp.int32)
    listing = members.reshape(top, rows).T
    listing = listing[jax.random.permutation(jax.random.fold_in(own, 1), rows)]
    offset_by = jax.random.randint(jax.random.fold_in(own, 2), (rows, 1), 0, top)
    return jnp.take_along_axis(listing, (jnp.arange(top)[None, :] + offset_by) % top, axis=1)


def portions_of(count, total, limit, skew, full):
    portions = [(1 << 20) // math.isqrt(standing ** skew) + 1 for standing in range(1, count + 1)]
    largest = limit if full else min(limit, max(-(-total // count), total * portions[0] // sum(portions)))
    least = 1 if total - largest >= count - 1 else 0
    counts, surplus = [largest] + [least] * (count - 1), total - largest - least * (count - 1)
    while surplus > 0:
        movable = [i for i in range(1, count) if counts[i] < largest] or [i for i in range(1, count) if counts[i] < limit]
        whole, left = sum([portions[i] for i in movable]), surplus
        for i in movable:
            more = min(limit - counts[i], max(1, left * portions[i] // whole), surplus)
            counts[i] = counts[i] + more
            surplus = surplus - more
    return np.array(counts)


def normal_values(key, extent, scale, bound, cuts=(), kind=jnp.bfloat16):
    factor_of = level_of(key, extent, cuts, -0.22, 0.18) if cuts else 1.0
    array = jax.random.normal(key, extent, jnp.float32) * scale * factor_of
    return jnp.minimum(jnp.maximum(array, -bound), bound).astype(kind)


def setup_inputs(seed: int = 0) -> dict:
    streams_of = jax.random.split(jax.random.key(seed), 8)
    traces = normal_values(streams_of[0], (OFFSETS, TRACES, NT), 1.0, 6.0, ((0, 8), (1, 64)))
    centre_ids_keys = jax.random.split(jax.random.fold_in(streams_of[1], 1), OFFSETS * TRACES // TRACE_DEV)
    centre_ids_turns = jax.random.permutation(jax.random.fold_in(streams_of[1], 3), OFFSETS * TRACES // TRACE_DEV)
    centre_ids = jax.vmap(lambda own, number: shared_out(jax.random.fold_in(streams_of[1], 2), own, number, TRACE_DEV, CENTRES, 1, CAP, 1))(centre_ids_keys, centre_ids_turns).reshape((OFFSETS, TRACES, 1))
    midpoint_bins = place_ends(jax.random.randint(streams_of[2], (OFFSETS, TRACES), 0, BINS), jax.random.fold_in(streams_of[2], 1), 0, BINS - 1).astype(jnp.int32)
    ray_times = jnp.clip(16.0 + 224.0 * jax.random.uniform(streams_of[3], (OFFSETS, CENTRES, WIN, P_SIZE, ZD), jnp.float32) ** level_of(streams_of[3], (OFFSETS, CENTRES, WIN, P_SIZE, ZD), ((0, 8), (1, 64)), -0.2, 0.2), 16.0, 240.0)
    ray_amps = jnp.clip(jnp.exp(math.log(2.0) - 2.3025851 * jax.random.uniform(streams_of[4], (OFFSETS, CENTRES, WIN, P_SIZE, ZD), jnp.float32) ** level_of(streams_of[4], (OFFSETS, CENTRES, WIN, P_SIZE, ZD), ((0, 8), (1, 64)), -0.2, 0.2)), 0.2, 2.0)
    beam_lateral = jnp.clip(128.0 * jax.random.uniform(streams_of[5], (OFFSETS, CENTRES, WIN, P_SIZE), jnp.float32) ** level_of(streams_of[5], (OFFSETS, CENTRES, WIN, P_SIZE), ((0, 8),), -0.2, 0.2), 0.0, 128.0)
    footprint = draw_footprint(jax.random.fold_in(streams_of[7], 71), 0)
    return {"traces": traces, "centre_ids": centre_ids, "midpoint_bins": midpoint_bins, "ray_times": ray_times, "ray_amps": ray_amps, "beam_lateral": beam_lateral, "footprint": footprint}


two_pi = 2.0 * math.pi
slow_step = 0.25
width_scale = 200.0

def dft_table():
    sample = jnp.arange(NT, dtype=jnp.int32)[:, None]
    bin_index = jnp.arange(NF, dtype=jnp.int32)[None, :] + KLO
    turns = (sample * bin_index % NT).astype(jnp.float32) * (two_pi / NT)
    return jnp.concatenate([jnp.cos(turns), -jnp.sin(turns)], axis=1)

def omegas():
    return (jnp.arange(NF, dtype=jnp.int32) + KLO).astype(jnp.float32) * (two_pi / NT)

def slowness():
    return (jnp.arange(P_SIZE, dtype=jnp.int32).astype(jnp.float32) - (P_SIZE - 1) / 2.0) * slow_step

def slant_terms(spectrum, places):
    phase = omegas()[None, None, :] * slowness()[None, :, None] * places[:, None, None]
    cosine = jnp.cos(phase)
    sine_part = jnp.sin(phase)
    spec_re = spectrum[:, None, :NF]
    spec_im = spectrum[:, None, NF:]
    return (spec_re * cosine + spec_im * sine_part, spec_im * cosine - spec_re * sine_part)

def beam_blocks(beams, times_in, amps_in, lateral, first_col, end_col):
    freq = omegas()
    phase = freq[None, :, None] * times_in[:, None, :]
    depth = times_in.shape[1]
    u_block = jnp.stack([amps_in[:, None, :] * jnp.cos(phase), -amps_in[:, None, :] * jnp.sin(phase)])
    u_block = u_block.reshape(2 * P_SIZE * NF, depth).astype(jnp.bfloat16)
    col_index = jnp.arange(XW, dtype=jnp.int32)
    inside = ((col_index >= first_col) & (col_index < end_col)).astype(jnp.float32)
    columns = col_index.astype(jnp.float32)
    gauss = jnp.exp(-(columns[None, None, :] - lateral[:, None, None]) ** 2 * freq[None, :, None] / width_scale)
    gauss = gauss * inside[None, None, :] / math.sqrt(P_SIZE * NF)
    beam_re = beams[:, :NF].astype(jnp.float32)[:, :, None]
    beam_im = beams[:, NF:].astype(jnp.float32)[:, :, None]
    v_block = jnp.stack([beam_re * gauss, beam_im * gauss]).reshape(2 * P_SIZE * NF, XW).astype(jnp.bfloat16)
    return (u_block, v_block)

def reference(traces, centre_ids, midpoint_bins, ray_times, ray_amps, beam_lateral, footprint):
    table = dft_table()
    half_win = (WIN - 1) // 2
    scale = 1.0 / math.sqrt(NT * TRACE_DEV)

    def one_group(group):
        group_traces, group_ids, group_bins, group_times, group_amps, group_lateral = group
        spectrum = jnp.dot(group_traces.astype(jnp.float32), table, precision=lax.Precision.HIGHEST)
        places = group_bins.astype(jnp.float32) - (BINS - 1) / 2.0
        terms_re, terms_im = slant_terms(spectrum, places)
        beam_re = jax.ops.segment_sum(terms_re, group_ids[:, 0], CENTRES)
        beam_im = jax.ops.segment_sum(terms_im, group_ids[:, 0], CENTRES)
        beams = (jnp.concatenate([beam_re, beam_im], axis=2) * scale).astype(jnp.bfloat16)

        def per_centre(centre, accum):
            for window in range(WIN):
                target = centre + window - half_win
                valid = ((target >= 0) & (target < CENTRES)).astype(jnp.float32)
                u_block, v_block = beam_blocks(beams[centre], group_times[centre, window], group_amps[centre, window], group_lateral[centre, window], footprint[centre, window, 0], footprint[centre, window, 1])
                contrib = lax.dot_general(u_block.astype(jnp.float32), v_block.astype(jnp.float32), (((0,), (0,)), ((), ())), precision=lax.Precision.HIGHEST)
                slot = jnp.clip(target, 0, CENTRES - 1).astype(jnp.int32)
                accum = accum.at[:, slot].add(contrib * valid)
            return accum
        start = jnp.zeros((ZD, CENTRES, XW), jnp.float32)
        return lax.fori_loop(0, CENTRES, per_centre, start)
    images = lax.map(one_group, (traces, centre_ids, midpoint_bins, ray_times, ray_amps, beam_lateral))
    return lax.optimization_barrier(jnp.sum(images, axis=0)).reshape(ZD, CENTRES * XW)
```

```python
import math

import jax
import jax.numpy as jnp
import numpy as np
from jax import lax
from jax.experimental import pallas as pl
from jax.experimental.pallas import tpu as pltpu
from jax.sharding import PartitionSpec as P

NT = 256
NF = 64
KLO = 8
P_SIZE = 16
BINS = 16
CAP = 6
WIN = 7
XW = 128
ROWS = 8
LANES = 128
HALF = (WIN - 1) // 2
KEEP = HALF + 1

two_pi = 2.0 * math.pi
slow_step = 0.25
width_scale = 200.0
omega_step = two_pi / NT

f32 = jnp.float32
bf16 = jnp.bfloat16


def dft_tables():
    sample = np.arange(NT)[:, None]
    turns = (sample * (np.arange(NF)[None, :] + KLO) % NT) * (two_pi / NT)
    table = np.concatenate([np.cos(turns), -np.sin(turns)], axis=1).astype(np.float32)
    high = table.astype(bf16)
    low = (table - high.astype(np.float32)).astype(bf16)
    return high, low


def slant_tables():
    freq = (np.arange(NF) + KLO) * omega_step
    slow = (np.arange(P_SIZE) - (P_SIZE - 1) / 2.0) * slow_step
    place = np.arange(BINS) - (BINS - 1) / 2.0
    phase = place[:, None, None] * freq[None, :, None] * slow[None, None, :]
    phase = phase.reshape(BINS, NF * P_SIZE)
    spread = np.arange(2 * NF)[:, None] % NF == np.arange(NF * P_SIZE)[None, :] // P_SIZE
    return (
        np.cos(phase).astype(np.float32),
        np.sin(phase).astype(np.float32),
        spread.astype(np.float32).astype(bf16),
    )


def iota(shape, dim):
    return lax.broadcasted_iota(jnp.int32, shape, dim)


def dot(a, b):
    return jnp.dot(a, b, preferred_element_type=f32)


def route_kernel(ids_ref, bins_ref, traces_ref, high_ref, low_ref, out_ref):
    count = traces_ref.shape[0]
    square = (count, count)
    row, col = iota(square, 0), iota(square, 1)
    ids_down = jnp.broadcast_to(ids_ref[...], square)
    ids_across = jnp.sum(jnp.where(row == col, ids_down, 0).astype(f32), axis=0, keepdims=True)
    ids_across = ids_across.astype(jnp.int32)
    same = ids_down == ids_across
    rank_across = jnp.sum(jnp.where(same & (row < col), 1.0, 0.0), axis=0, keepdims=True)
    rank_down = jnp.sum(jnp.where(same & (col < row), 1.0, 0.0), axis=1, keepdims=True)
    place_across = bins_ref[...].astype(f32) - (BINS - 1) / 2.0
    place_down = jnp.sum(jnp.where(row == col, place_across, 0.0), axis=1, keepdims=True)
    traces = traces_ref[...]
    spectrum = dot(traces, high_ref[...]) + dot(traces, low_ref[...])
    places = jnp.where(col == rank_down.astype(jnp.int32), place_down, 0.0)
    values = jnp.concatenate([spectrum, places], axis=1).astype(bf16)
    out_rows = out_ref.shape[0]
    slot = iota((out_rows, count), 0)
    place_row = slot % ROWS == CAP
    target = ids_across * ROWS + rank_across.astype(jnp.int32)
    pick = (slot == target) | (place_row & (slot // ROWS == ids_across))
    picked = dot(jnp.where(pick, 1.0, 0.0).astype(bf16), values)
    out_ref[...] = jnp.where(place_row, picked[:, LANES:], picked[:, :LANES]).astype(bf16)


def slant_stack(arrived, spread, cosine, sine, scale):
    rows = arrived.shape[0]
    full = arrived.astype(f32).reshape(rows // ROWS, ROWS, LANES)
    sub, lane = iota((rows // ROWS, ROWS, LANES), 1), iota((rows // ROWS, ROWS, LANES), 2)
    own = jnp.where(sub == lane, jnp.broadcast_to(full[:, CAP : CAP + 1, :], full.shape), 0.0)
    own = own.reshape(rows, LANES).astype(bf16)
    place = dot(own, jnp.ones((LANES, LANES), bf16))
    bin_place = iota((rows, LANES), 1).astype(f32) - (BINS - 1) / 2.0
    in_bin = jnp.where((place == bin_place) & (place != 0.0), 1.0, 0.0).astype(bf16)
    binned = lax.dot_general(
        in_bin, arrived, (((0,), (0,)), ((), ())), preferred_element_type=f32
    )[:BINS]
    real = iota((BINS, LANES), 1) < NF
    binned_re = jnp.where(real, binned, 0.0)
    binned_im = jnp.where(real, 0.0, binned)
    parts = []
    for part in (binned_re, binned_im):
        high = part.astype(bf16)
        parts += [high, (part - high.astype(f32)).astype(bf16)]
    wide = dot(jnp.concatenate(parts, axis=0), spread)
    wide_re = wide[:BINS] + wide[BINS : 2 * BINS]
    wide_im = wide[2 * BINS : 3 * BINS] + wide[3 * BINS :]
    beam_re = jnp.sum(wide_re * cosine + wide_im * sine, axis=0, keepdims=True)
    beam_im = jnp.sum(wide_im * cosine - wide_re * sine, axis=0, keepdims=True)
    return (
        (beam_re * scale).astype(bf16).astype(f32),
        (beam_im * scale).astype(bf16).astype(f32),
    )


def cos_sin_turns(turns):
    half = (turns - 0.5) * math.pi
    sq = half * half
    sin_of = 1.0 / 6227020800.0
    for divisor in (-39916800.0, 362880.0, -5040.0, 120.0, -6.0, 1.0):
        sin_of = sin_of * sq + 1.0 / divisor
    sin_of = sin_of * half
    cos_of = 1.0 / 479001600.0
    for divisor in (-3628800.0, 40320.0, -720.0, 24.0, -2.0, 1.0):
        cos_of = cos_of * sq + 1.0 / divisor
    return 2.0 * sin_of * sin_of - 1.0, -2.0 * sin_of * cos_of


def fill_u(u_ref, times, amps):
    cos_1, sin_1 = cos_sin_turns(times * (1.0 / NT))
    power = (cos_1, sin_1)

    def times_of(a, b):
        return a[0] * b[0] - a[1] * b[1], a[0] * b[1] + a[1] * b[0]

    one = power
    two = times_of(one, one)
    four = times_of(two, two)
    eight = times_of(four, four)
    start = (amps * eight[0], amps * eight[1])
    walk = [start]
    walk.append(times_of(start, one))
    walk.append(times_of(start, two))
    walk.append(times_of(walk[1], two))
    values = [(c, -s) for c, s in walk]
    factor = 2.0 * two[0]
    for j in range(NF):
        if j >= 4:
            values.append(
                tuple(factor * values[j - 2][i] - values[j - 4][i] for i in range(2))
            )
        group, inner = divmod(j, LANES // P_SIZE)
        for i in range(2):
            first = group * 2 * LANES + i * LANES + inner * P_SIZE
            u_ref[pl.ds(first, P_SIZE), :] = values[j][i].astype(bf16)


def migrate_kernel(
    core_ref, foot_ref, arrived_ref, lateral_ref, times_ref, amps_ref, spread_ref, cos_ref, sin_ref,
    keep_ref, give_ref, u_ref, v_ref, *, scale,
):
    core = core_ref[0]
    beam_re, beam_im = slant_stack(
        arrived_ref[...], spread_ref[...], cos_ref[...], sin_ref[...], scale
    )
    xs = iota((XW, LANES), 0)
    columns = xs.astype(f32)
    first_freq = (iota((XW, LANES), 1) // P_SIZE + KLO).astype(f32) * (omega_step / width_scale)
    group_freq = (LANES // P_SIZE) * omega_step / width_scale
    outputs, depth = keep_ref.shape[0], keep_ref.shape[2]

    def contribution(w):
        fill_u(u_ref, times_ref[w], amps_ref[w])
        away = columns - lateral_ref[pl.ds(w, 1), :]
        minus = -(away * away)
        inside = (xs >= foot_ref[w, 0]) & (xs < foot_ref[w, 1])
        gauss = jnp.where(inside, jnp.exp(minus * first_freq), 0.0) * (
            1.0 / math.sqrt(P_SIZE * NF)
        )
        ratio = jnp.exp(minus * group_freq)
        for group in range(NF * P_SIZE // LANES):
            lanes = slice(group * LANES, (group + 1) * LANES)
            v_ref[:, 2 * group * LANES : (2 * group + 1) * LANES] = (
                gauss * beam_re[:, lanes]
            ).astype(bf16)
            v_ref[:, (2 * group + 1) * LANES : (2 * group + 2) * LANES] = (
                gauss * beam_im[:, lanes]
            ).astype(bf16)
            gauss = gauss * ratio
        return dot(v_ref[...], u_ref[...]).T

    def give_step(q, carry):
        w = jnp.where(core == 0, KEEP + q, HALF - 1 - q)
        result = contribution(w).astype(bf16)
        for o in range(outputs):
            give_ref[o, q] = result[o * depth : (o + 1) * depth]
        return carry

    def keep_step(q, carry):
        w = jnp.where(core == 0, HALF - q, HALF + q)
        result = contribution(w)
        for o in range(outputs):
            keep_ref[o, q] = result[o * depth : (o + 1) * depth]
        return carry

    lax.fori_loop(0, HALF, give_step, 0)
    lax.fori_loop(0, KEEP, keep_step, 0)


def merge_kernel(keep_ref, taken_ref, out_ref):
    out_ref[:, :HALF] = (keep_ref[:, :HALF] + taken_ref[...].astype(f32)).astype(bf16)
    out_ref[:, HALF:] = keep_ref[:, HALF:].astype(bf16)


def total_kernel(parts_ref, *out_refs):
    for q, out_ref in enumerate(out_refs):
        total = parts_ref[0, q].astype(f32)
        for o in range(1, parts_ref.shape[0]):
            total = total + parts_ref[o, q].astype(f32)
        out_ref[...] = total


def vmem():
    return pl.BlockSpec(memory_space=pltpu.VMEM)


def smem():
    return pl.BlockSpec(memory_space=pltpu.SMEM)


def shards(traces, centre_ids, midpoint_bins, ray_times, ray_amps, beam_lateral, footprint):
    my_slab = lax.axis_index("slab")
    slabs = lax.axis_size("slab")
    offsets = lax.axis_size("offset")
    count = traces.shape[1]
    depth = ray_times.shape[4]
    part = depth // offsets
    high, low = dft_tables()
    routed = pl.pallas_call(
        route_kernel,
        out_shape=jax.ShapeDtypeStruct((slabs * ROWS, LANES), bf16),
        in_specs=[vmem()] * 5,
        out_specs=vmem(),
    )(centre_ids[0], midpoint_bins, traces[0], jnp.asarray(high), jnp.asarray(low))
    arrived = lax.all_to_all(
        routed.reshape(slabs, ROWS, LANES), "slab", split_axis=0, concat_axis=0, tiled=True
    ).reshape(slabs * ROWS, LANES)

    lateral = lax.dynamic_index_in_dim(beam_lateral[0], my_slab, 0, keepdims=False)
    lateral = jnp.tile(lateral, (1, LANES // P_SIZE))
    foot = lax.dynamic_index_in_dim(footprint, my_slab, 0, keepdims=False)
    core = (my_slab % 2).astype(jnp.int32).reshape(1)
    cosine, sine, spread = slant_tables()
    keep, give = pl.pallas_call(
        lambda *refs: migrate_kernel(*refs, scale=1.0 / math.sqrt(NT * count)),
        out_shape=(
            jax.ShapeDtypeStruct((offsets, KEEP, part, XW), f32),
            jax.ShapeDtypeStruct((offsets, HALF, part, XW), bf16),
        ),
        in_specs=[smem(), smem()] + [vmem()] * 7,
        out_specs=(vmem(), vmem()),
        scratch_shapes=[
            pltpu.VMEM((2 * P_SIZE * NF, depth), bf16),
            pltpu.VMEM((XW, 2 * P_SIZE * NF), bf16),
        ],
        compiler_params=pltpu.CompilerParams(vmem_limit_bytes=32 * 1024 * 1024),
    )(
        core, foot, arrived, lateral, ray_times[0, 0], ray_amps[0, 0],
        jnp.asarray(spread), jnp.asarray(cosine), jnp.asarray(sine),
    )
    swap = [(i, i ^ 1) for i in range(slabs)]
    taken = lax.ppermute(give, "slab", swap)
    merged = pl.pallas_call(
        merge_kernel,
        out_shape=jax.ShapeDtypeStruct((offsets, KEEP, part, XW), bf16),
        in_specs=[vmem()] * 2,
        out_specs=vmem(),
    )(keep, taken)
    parts = lax.all_to_all(merged, "offset", split_axis=0, concat_axis=0, tiled=True)
    totals = pl.pallas_call(
        total_kernel,
        out_shape=tuple(jax.ShapeDtypeStruct((part, XW), f32) for _ in range(KEEP)),
        in_specs=[vmem()],
        out_specs=tuple(vmem() for _ in range(KEEP)),
    )(parts)
    image = totals[0]
    for step in range(1, KEEP):
        pairs = [(i, i - step if i % 2 == 0 else i + step) for i in range(slabs)]
        pairs = [(i, j) for i, j in pairs if 0 <= j < slabs]
        image = image + lax.ppermute(totals[step], "slab", pairs)
    return image


def solution(mesh):
    return jax.shard_map(
        shards,
        mesh=mesh,
        in_specs=(
            P("offset", "slab", None),
            P("offset", "slab", None),
            P("offset", "slab"),
            P("offset", "slab", None, None, None),
            P("offset", "slab", None, None, None),
            P("offset", None, None, None),
            P(),
        ),
        out_specs=P("offset", "slab"),
        check_vma=False,
    )
```

```python
import math

import jax
import jax.numpy as jnp
import numpy as np
from jax import lax
from jax.experimental import pallas as pl
from jax.experimental.pallas import tpu as pltpu
from jax.sharding import Mesh
from jax.sharding import PartitionSpec as P

NT = 256
NF = 64
KLO = 8
P_SIZE = 16
BINS = 16
CAP = 6
WIN = 7
XW = 128
ROWS = 8
LANES = 128
HALF = (WIN - 1) // 2
GROUPS = P_SIZE * NF // LANES

two_pi = 2.0 * math.pi
slow_step = 0.25
width_scale = 200.0
omega_step = two_pi / NT

f32 = jnp.float32
bf16 = jnp.bfloat16


def dft_tables():
    sample = np.arange(NT)[:, None]
    turns = (sample * (np.arange(NF)[None, :] + KLO) % NT) * (two_pi / NT)
    table = np.concatenate([np.cos(turns), -np.sin(turns)], axis=1).astype(np.float32)
    high = table.astype(bf16)
    low = (table - high.astype(np.float32)).astype(bf16)
    return high, low


def slant_tables():
    freq = (np.arange(NF) + KLO) * omega_step
    slow = (np.arange(P_SIZE) - (P_SIZE - 1) / 2.0) * slow_step
    place = np.arange(BINS) - (BINS - 1) / 2.0
    phase = place[:, None, None] * freq[None, :, None] * slow[None, None, :]
    phase = phase.reshape(BINS, NF * P_SIZE)
    spread = np.arange(2 * NF)[:, None] % NF == np.arange(NF * P_SIZE)[None, :] // P_SIZE
    return (
        np.cos(phase).astype(np.float32),
        np.sin(phase).astype(np.float32),
        spread.astype(np.float32).astype(bf16),
    )


def iota(shape, dim):
    return lax.broadcasted_iota(jnp.int32, shape, dim)


def dot(a, b):
    return jnp.dot(a, b, preferred_element_type=f32)


def route_kernel(ids_ref, bins_ref, traces_ref, high_ref, low_ref, out_ref):
    count = traces_ref.shape[0]
    square = (count, count)
    row, col = iota(square, 0), iota(square, 1)
    ids_across = ids_ref[...]
    ids_down = jnp.sum(
        jnp.where(row == col, ids_across.astype(f32), 0.0), axis=1, keepdims=True
    )
    same = ids_down == ids_across.astype(f32)
    rank_across = jnp.sum(jnp.where(same & (row < col), 1.0, 0.0), axis=0, keepdims=True)
    rank_down = jnp.sum(jnp.where(same & (col < row), 1.0, 0.0), axis=1, keepdims=True)
    place_across = bins_ref[...].astype(f32) - (BINS - 1) / 2.0
    place_down = jnp.sum(jnp.where(row == col, place_across, 0.0), axis=1, keepdims=True)
    traces = traces_ref[...]
    spectrum = dot(traces, high_ref[...]) + dot(traces, low_ref[...])
    places = jnp.where(col == rank_down.astype(jnp.int32), place_down, 0.0)
    values = jnp.concatenate([spectrum, places], axis=1).astype(bf16)
    out_rows = out_ref.shape[0]
    slot = iota((out_rows, count), 0)
    place_row = slot % ROWS == CAP
    target = ids_across * ROWS + rank_across.astype(jnp.int32)
    pick = (slot == target) | (place_row & (slot // ROWS == ids_across))
    picked = dot(jnp.where(pick, 1.0, 0.0).astype(bf16), values)
    out_ref[...] = jnp.where(place_row, picked[:, LANES:], picked[:, :LANES]).astype(bf16)


def slant_stack(arrived, spread, cosine, sine, scale):
    rows = arrived.shape[0]
    full = arrived.astype(f32).reshape(rows // ROWS, ROWS, LANES)
    sub, lane = iota((rows // ROWS, ROWS, LANES), 1), iota((rows // ROWS, ROWS, LANES), 2)
    own = jnp.where(sub == lane, jnp.broadcast_to(full[:, CAP : CAP + 1, :], full.shape), 0.0)
    own = own.reshape(rows, LANES).astype(bf16)
    place = dot(own, jnp.ones((LANES, LANES), bf16))
    bin_place = iota((rows, LANES), 1).astype(f32) - (BINS - 1) / 2.0
    in_bin = jnp.where((place == bin_place) & (place != 0.0), 1.0, 0.0).astype(bf16)
    binned = lax.dot_general(
        in_bin, arrived, (((0,), (0,)), ((), ())), preferred_element_type=f32
    )[:BINS]
    real = iota((BINS, LANES), 1) < NF
    binned_re = jnp.where(real, binned, 0.0)
    binned_im = jnp.where(real, 0.0, binned)
    parts = []
    for part in (binned_re, binned_im):
        high = part.astype(bf16)
        parts += [high, (part - high.astype(f32)).astype(bf16)]
    wide = dot(jnp.concatenate(parts, axis=0), spread)
    wide_re = wide[:BINS] + wide[BINS : 2 * BINS]
    wide_im = wide[2 * BINS : 3 * BINS] + wide[3 * BINS :]
    beam_re = jnp.sum(wide_re * cosine + wide_im * sine, axis=0, keepdims=True)
    beam_im = jnp.sum(wide_im * cosine - wide_re * sine, axis=0, keepdims=True)
    return (
        (beam_re * scale).astype(bf16).astype(f32),
        (beam_im * scale).astype(bf16).astype(f32),
    )


def cos_sin_turns(turns):
    half = (turns - 0.5) * math.pi
    sq = half * half
    sin_of = 1.0 / 6227020800.0
    for divisor in (-39916800.0, 362880.0, -5040.0, 120.0, -6.0, 1.0):
        sin_of = sin_of * sq + 1.0 / divisor
    sin_of = sin_of * half
    cos_of = 1.0 / 479001600.0
    for divisor in (-3628800.0, 40320.0, -720.0, 24.0, -2.0, 1.0):
        cos_of = cos_of * sq + 1.0 / divisor
    return 2.0 * sin_of * sin_of - 1.0, -2.0 * sin_of * cos_of


def u_groups(u_ref, times, amps):
    def times_of(a, b):
        return a[0] * b[0] - a[1] * b[1], a[0] * b[1] + a[1] * b[0]

    one = cos_sin_turns(times * (1.0 / NT))
    two = times_of(one, one)
    four = times_of(two, two)
    eight = times_of(four, four)
    start = (amps * eight[0], amps * eight[1])
    walk = [start, times_of(start, one), times_of(start, two)]
    walk.append(times_of(walk[1], two))
    values = [(c, -s) for c, s in walk]
    factor = 2.0 * two[0]
    for j in range(NF):
        if j >= 4:
            values.append(
                tuple(factor * values[j - 2][i] - values[j - 4][i] for i in range(2))
            )
        group, inner = divmod(j, LANES // P_SIZE)
        for i in range(2):
            first = group * 2 * LANES + i * LANES + inner * P_SIZE
            u_ref[pl.ds(first, P_SIZE), :] = values[j][i].astype(bf16)
        if inner == LANES // P_SIZE - 1:
            yield


def v_groups(w, beam_re, beam_im, foot_ref, lateral_ref):
    xs = iota((XW, LANES), 0)
    freq = (iota((XW, LANES), 1) // P_SIZE + KLO).astype(f32) * (omega_step / width_scale)
    away = xs.astype(f32) - lateral_ref[pl.ds(w, 1), :]
    minus = -(away * away)
    inside = (xs >= foot_ref[w, 0]) & (xs < foot_ref[w, 1])
    gauss = jnp.where(inside, jnp.exp(minus * freq), 0.0) * (1.0 / math.sqrt(P_SIZE * NF))
    ratio = jnp.exp(minus * ((LANES // P_SIZE) * omega_step / width_scale))
    for group in range(GROUPS):
        lanes = slice(group * LANES, (group + 1) * LANES)
        yield jnp.concatenate(
            [(gauss * beam_re[:, lanes]).astype(bf16), (gauss * beam_im[:, lanes]).astype(bf16)],
            axis=1,
        )
        gauss = gauss * ratio


def contributions(windows, beams_of, foot_ref, lateral_ref, times_ref, amps_ref, u_ref, store):
    def u_of(i):
        return u_groups(u_ref.at[i], times_ref[windows[i]], amps_ref[windows[i]])

    for _ in u_of(0):
        pass
    beam_re, beam_im = beams_of()
    for i, w in enumerate(windows):
        following = u_of(i + 1) if i + 1 < len(windows) else iter(())
        total = None
        for group, v in enumerate(v_groups(w, beam_re, beam_im, foot_ref, lateral_ref)):
            part = dot(v, u_ref[i, pl.ds(group * 2 * LANES, 2 * LANES), :])
            total = part if total is None else total + part
            next(following, None)
        store(i, total.T)


def far_kernel(
    place_ref, foot_ref, arrived_ref, lateral_ref, times_ref, amps_ref, spread_ref, cos_ref,
    sin_ref, seam_ref, pair_ref, outer_ref, beam_ref, u_ref, *, scale,
):
    core, odd = place_ref[0], place_ref[1]

    def beams_of():
        beams = slant_stack(
            arrived_ref[...], spread_ref[...], cos_ref[...], sin_ref[...], scale
        )
        for i in range(2):
            beam_ref[i : i + 1] = beams[i]
        return beams

    def store(i, block):
        block = block.astype(bf16)
        if i < 3:
            seam_ref[i] = block
        else:
            pair_ref[i - 3] = block
        if i == 2:
            outer_ref[...] = block

    left, right = 1 - core, 5 - core
    to_seam, to_pair = jnp.where(odd == 0, left, right), jnp.where(odd == 0, right, left)
    windows = [to_seam, to_seam + 1, core * (WIN - 1), to_pair, to_pair + 1]
    contributions(windows, beams_of, foot_ref, lateral_ref, times_ref, amps_ref, u_ref, store)


def near_kernel(
    place_ref, foot_ref, beam_ref, lateral_ref, times_ref, amps_ref, near_ref, u_ref
):
    def store(i, block):
        near_ref[i] = block

    first = HALF - place_ref[0]
    contributions(
        [first, first + 1], lambda: (beam_ref[0:1], beam_ref[1:2]),
        foot_ref, lateral_ref, times_ref, amps_ref, u_ref, store,
    )


def merge_kernel(place_ref, near_ref, seam_ref, pair_ref, outer_ref, last_ref, out_ref):
    core = place_ref[0]
    cores, rows = 2, out_ref.shape[1]
    outer = outer_ref[...].astype(f32) + last_ref[...].astype(f32)
    for i in range(cores):
        total = near_ref[i] + seam_ref[i].astype(f32) + pair_ref[i].astype(f32)
        total = (total + jnp.where(core == i, outer, 0.0)).astype(bf16)
        for o in range(out_ref.shape[0] // cores):
            out_ref[o * cores + i] = total[o * rows : (o + 1) * rows]


def total_kernel(parts_ref, out_ref):
    total = parts_ref[0].astype(f32)
    for i in range(1, parts_ref.shape[0]):
        total = total + parts_ref[i].astype(f32)
    out_ref[...] = total


def vmem():
    return pl.BlockSpec(memory_space=pltpu.VMEM)


def smem():
    return pl.BlockSpec(memory_space=pltpu.SMEM)


def call(kernel, out_shape, in_specs, mib=None, scratch=(), flops=0):
    many = isinstance(out_shape, tuple)
    limit = None if mib is None else mib * 1024 * 1024
    return pl.pallas_call(
        kernel,
        out_shape=out_shape,
        in_specs=in_specs,
        out_specs=tuple(vmem() for _ in out_shape) if many else vmem(),
        scratch_shapes=scratch,
        compiler_params=pltpu.CompilerParams(vmem_limit_bytes=limit),
        cost_estimate=pl.CostEstimate(flops=flops, bytes_accessed=1 << 20, transcendentals=0),
    )


def struct(*shape):
    return jax.ShapeDtypeStruct(shape, bf16)


def struct32(*shape):
    return jax.ShapeDtypeStruct(shape, f32)


def shards(traces, centre_ids, midpoint_bins, ray_times, ray_amps, beam_lateral, footprint):
    slab_axes = ("chip", "core")
    my_slab = lax.axis_index(slab_axes)
    slabs = lax.axis_size(slab_axes)
    offsets = lax.axis_size("offset")
    count = traces.shape[1]
    depth = ray_times.shape[4]
    part = depth // offsets
    high, low = dft_tables()
    routed = call(route_kernel, struct(slabs * ROWS, LANES), [vmem()] * 5)(
        centre_ids.reshape(1, count), midpoint_bins, traces[0], jnp.asarray(high), jnp.asarray(low)
    )
    arrived = lax.all_to_all(
        routed.reshape(slabs, ROWS, LANES), slab_axes, split_axis=0, concat_axis=0, tiled=True
    ).reshape(slabs * ROWS, LANES)

    lateral = lax.dynamic_index_in_dim(beam_lateral[0], my_slab, 0, keepdims=False)
    lateral = jnp.tile(lateral, (1, LANES // P_SIZE))
    foot = lax.dynamic_index_in_dim(footprint, my_slab, 0, keepdims=False)
    u_rows = 2 * P_SIZE * NF
    place = jnp.stack([my_slab % 2, my_slab // 2 % 2]).astype(jnp.int32)
    cosine, sine, spread = slant_tables()
    to_seam, to_pair, to_outer, beams = call(
        lambda *refs: far_kernel(*refs, scale=1.0 / math.sqrt(NT * count)),
        (struct(3, depth, XW), struct(2, depth, XW), struct(depth, XW), struct32(2, NF * P_SIZE)),
        [smem()] * 2 + [vmem()] * 7,
        24,
        [pltpu.VMEM((WIN - 2, u_rows, depth), bf16)],
    )(
        place, foot, arrived, lateral, ray_times[0, 0], ray_amps[0, 0],
        jnp.asarray(spread), jnp.asarray(cosine), jnp.asarray(sine),
    )

    half = slabs // 2

    def chip_pairs(parity):
        pairs = [(i, i + 2 if i // 2 % 2 == parity else i - 2) for i in range(slabs)]
        return [(i, j) for i, j in pairs if 0 <= j < slabs]

    outward = [(i, i + 3 if i % 2 else i - 3) for i in range(slabs)]
    outward = [(i, j) for i, j in outward if 0 <= j < slabs and i not in (half - 1, half)]
    from_seam = lax.ppermute(to_seam, slab_axes, chip_pairs(1))
    from_pair = lax.ppermute(to_pair, slab_axes, chip_pairs(0))
    from_outer = lax.ppermute(to_outer, slab_axes, outward)
    near = call(
        near_kernel,
        struct32(2, depth, XW),
        [smem()] * 2 + [vmem()] * 4,
        24,
        [pltpu.VMEM((2, u_rows, depth), bf16)],
        flops=1 << 28,
    )(place, foot, beams, lateral, ray_times[0, 0], ray_amps[0, 0])
    last = lax.ppermute(from_seam[2], slab_axes, [(half - 2, half - 3), (half + 1, half + 2)])
    merged = call(merge_kernel, struct(2 * offsets, part, XW), [smem()] + [vmem()] * 5, 8)(
        place, near, from_seam, from_pair, from_outer, last
    )
    parts = lax.all_to_all(
        merged, ("offset", "core"), split_axis=0, concat_axis=0, tiled=True
    )
    return call(total_kernel, struct32(part, XW), [vmem()], 4)(parts)


def solution(mesh):
    offsets, slabs = mesh.devices.shape
    chips = Mesh(mesh.devices.reshape(offsets, slabs // 2, 2), ("offset", "chip", "core"))
    slab = ("chip", "core")
    return jax.shard_map(
        shards,
        mesh=chips,
        in_specs=(
            P("offset", slab, None),
            P("offset", slab, None),
            P("offset", slab),
            P("offset", slab, None, None, None),
            P("offset", slab, None, None, None),
            P("offset", None, None, None),
            P(),
        ),
        out_specs=P("offset", slab),
        check_vma=False,
    )
```

```python
import math

import jax
import jax.numpy as jnp
import numpy as np
from jax import lax
from jax.experimental import pallas as pl
from jax.experimental.pallas import tpu as pltpu
from jax.sharding import Mesh
from jax.sharding import PartitionSpec as P

NT = 256
NF = 64
KLO = 8
P_SIZE = 16
BINS = 16
CAP = 6
WIN = 7
XW = 128
ROWS = 8
LANES = 128
HALF = (WIN - 1) // 2
GROUPS = P_SIZE * NF // LANES
GROUP = 4

two_pi = 2.0 * math.pi
slow_step = 0.25
width_scale = 200.0
omega_step = two_pi / NT

f32 = jnp.float32
bf16 = jnp.bfloat16


def dft_tables():
    sample = np.arange(NT)[:, None]
    turns = (sample * (np.arange(NF)[None, :] + KLO) % NT) * (two_pi / NT)
    table = np.concatenate([np.cos(turns), -np.sin(turns)], axis=1).astype(np.float32)
    high = table.astype(bf16)
    low = (table - high.astype(np.float32)).astype(bf16)
    return high, low


def slant_tables():
    freq = (np.arange(NF) + KLO) * omega_step
    slow = (np.arange(P_SIZE) - (P_SIZE - 1) / 2.0) * slow_step
    place = np.arange(BINS) - (BINS - 1) / 2.0
    phase = place[:, None, None] * freq[None, :, None] * slow[None, None, :]
    phase = phase.reshape(BINS, NF * P_SIZE)
    spread = np.arange(2 * NF)[:, None] % NF == np.arange(NF * P_SIZE)[None, :] // P_SIZE
    return (
        np.cos(phase).astype(np.float32),
        np.sin(phase).astype(np.float32),
        spread.astype(np.float32).astype(bf16),
    )


def iota(shape, dim):
    return lax.broadcasted_iota(jnp.int32, shape, dim)


def dot(a, b):
    return jnp.dot(a, b, preferred_element_type=f32)


def route_kernel(ids_ref, bins_ref, traces_ref, high_ref, low_ref, out_ref):
    count = traces_ref.shape[0]
    square = (count, count)
    row, col = iota(square, 0), iota(square, 1)
    ids_across = ids_ref[...]
    ids_down = jnp.sum(
        jnp.where(row == col, ids_across.astype(f32), 0.0), axis=1, keepdims=True
    )
    same = ids_down == ids_across.astype(f32)
    rank_across = jnp.sum(jnp.where(same & (row < col), 1.0, 0.0), axis=0, keepdims=True)
    rank_down = jnp.sum(jnp.where(same & (col < row), 1.0, 0.0), axis=1, keepdims=True)
    place_across = bins_ref[...].astype(f32) - (BINS - 1) / 2.0
    place_down = jnp.sum(jnp.where(row == col, place_across, 0.0), axis=1, keepdims=True)
    traces = traces_ref[...]
    spectrum = dot(traces, high_ref[...]) + dot(traces, low_ref[...])
    places = jnp.where(col == rank_down.astype(jnp.int32), place_down, 0.0)
    values = jnp.concatenate([spectrum, places], axis=1).astype(bf16)
    out_rows = out_ref.shape[0]
    slot = iota((out_rows, count), 0)
    place_row = slot % ROWS == CAP
    target = ids_across * ROWS + rank_across.astype(jnp.int32)
    pick = (slot == target) | (place_row & (slot // ROWS == ids_across))
    picked = dot(jnp.where(pick, 1.0, 0.0).astype(bf16), values)
    out_ref[...] = jnp.where(place_row, picked[:, LANES:], picked[:, :LANES]).astype(bf16)


def slant_stack(arrived, spread, cosine, sine, scale):
    rows = arrived.shape[0]
    full = arrived.astype(f32).reshape(rows // ROWS, ROWS, LANES)
    sub, lane = iota((rows // ROWS, ROWS, LANES), 1), iota((rows // ROWS, ROWS, LANES), 2)
    own = jnp.where(sub == lane, jnp.broadcast_to(full[:, CAP : CAP + 1, :], full.shape), 0.0)
    own = own.reshape(rows, LANES).astype(bf16)
    place = dot(own, jnp.ones((LANES, LANES), bf16))
    bin_place = iota((rows, LANES), 1).astype(f32) - (BINS - 1) / 2.0
    in_bin = jnp.where((place == bin_place) & (place != 0.0), 1.0, 0.0).astype(bf16)
    binned = lax.dot_general(
        in_bin, arrived, (((0,), (0,)), ((), ())), preferred_element_type=f32
    )[:BINS]
    real = iota((BINS, LANES), 1) < NF
    binned_re = jnp.where(real, binned, 0.0)
    binned_im = jnp.where(real, 0.0, binned)
    parts = []
    for part in (binned_re, binned_im):
        high = part.astype(bf16)
        parts += [high, (part - high.astype(f32)).astype(bf16)]
    wide = dot(jnp.concatenate(parts, axis=0), spread)
    wide_re = wide[:BINS] + wide[BINS : 2 * BINS]
    wide_im = wide[2 * BINS : 3 * BINS] + wide[3 * BINS :]
    beam_re = jnp.sum(wide_re * cosine + wide_im * sine, axis=0, keepdims=True)
    beam_im = jnp.sum(wide_im * cosine - wide_re * sine, axis=0, keepdims=True)
    return (
        (beam_re * scale).astype(bf16).astype(f32),
        (beam_im * scale).astype(bf16).astype(f32),
    )


def cos_sin_turns(turns):
    half = (turns - 0.5) * math.pi
    sq = half * half
    sin_of = 1.0 / 6227020800.0
    for divisor in (-39916800.0, 362880.0, -5040.0, 120.0, -6.0, 1.0):
        sin_of = sin_of * sq + 1.0 / divisor
    sin_of = sin_of * half
    cos_of = 1.0 / 479001600.0
    for divisor in (-3628800.0, 40320.0, -720.0, 24.0, -2.0, 1.0):
        cos_of = cos_of * sq + 1.0 / divisor
    return 2.0 * sin_of * sin_of - 1.0, -2.0 * sin_of * cos_of


def u_groups(u_ref, times, amps):
    def times_of(a, b):
        return a[0] * b[0] - a[1] * b[1], a[0] * b[1] + a[1] * b[0]

    one = cos_sin_turns(times * (1.0 / NT))
    two = times_of(one, one)
    four = times_of(two, two)
    eight = times_of(four, four)
    start = (amps * eight[0], amps * eight[1])
    walk = [start, times_of(start, one), times_of(start, two)]
    walk.append(times_of(walk[1], two))
    values = [(c, -s) for c, s in walk]
    factor = 2.0 * two[0]
    for j in range(NF):
        if j >= 4:
            values.append(
                tuple(factor * values[j - 2][i] - values[j - 4][i] for i in range(2))
            )
        group, inner = divmod(j, LANES // P_SIZE)
        for i in range(2):
            first = group * 2 * LANES + i * LANES + inner * P_SIZE
            u_ref[pl.ds(first, P_SIZE), :] = values[j][i].astype(bf16)
        if inner == LANES // P_SIZE - 1:
            yield


def v_groups(w, beam_re, beam_im, foot_ref, lateral_ref):
    xs = iota((XW, LANES), 0)
    freq = (iota((XW, LANES), 1) // P_SIZE + KLO).astype(f32) * (omega_step / width_scale)
    away = xs.astype(f32) - lateral_ref[pl.ds(w, 1), :]
    minus = -(away * away)
    inside = (xs >= foot_ref[w, 0]) & (xs < foot_ref[w, 1])
    gauss = jnp.where(inside, jnp.exp(minus * freq), 0.0) * (1.0 / math.sqrt(P_SIZE * NF))
    ratio = jnp.exp(minus * ((LANES // P_SIZE) * omega_step / width_scale))
    for group in range(GROUPS):
        lanes = slice(group * LANES, (group + 1) * LANES)
        yield jnp.concatenate(
            [(gauss * beam_re[:, lanes]).astype(bf16), (gauss * beam_im[:, lanes]).astype(bf16)],
            axis=1,
        )
        gauss = gauss * ratio


def contributions(windows, beams_of, foot_ref, lateral_ref, times_ref, amps_ref, u_ref, store):
    def u_of(i):
        return u_groups(u_ref.at[i], times_ref[windows[i]], amps_ref[windows[i]])

    for _ in u_of(0):
        pass
    beam_re, beam_im = beams_of()
    for i, w in enumerate(windows):
        following = u_of(i + 1) if i + 1 < len(windows) else iter(())
        total = None
        for group, v in enumerate(v_groups(w, beam_re, beam_im, foot_ref, lateral_ref)):
            part = dot(v, u_ref[i, pl.ds(group * 2 * LANES, 2 * LANES), :])
            total = part if total is None else total + part
            next(following, None)
        store(i, total.T)


def far_kernel(
    place_ref, foot_ref, arrived_ref, lateral_ref, times_ref, amps_ref, spread_ref, cos_ref,
    sin_ref, seam_ref, outer_ref, beam_ref, u_ref, *, scale,
):
    place = place_ref[0]

    def beams_of():
        beams = slant_stack(
            arrived_ref[...], spread_ref[...], cos_ref[...], sin_ref[...], scale
        )
        for i in range(2):
            beam_ref[i : i + 1] = beams[i]
        return beams

    def store(i, block):
        block = block.astype(bf16)
        is_outer = place == {0: 1, 1: -1, 2: 2}[i]
        seam_ref[i] = jnp.where(is_outer, jnp.zeros_like(block), block)
        if i != 1:

            @pl.when(is_outer | (i == 0))
            def _():
                outer_ref[...] = block

    windows = [(i - place + WIN) % WIN for i in range(HALF)]
    contributions(windows, beams_of, foot_ref, lateral_ref, times_ref, amps_ref, u_ref, store)


def near_kernel(
    place_ref, foot_ref, beam_ref, lateral_ref, times_ref, amps_ref, near_ref, u_ref
):
    def store(i, block):
        near_ref[i] = block

    first = HALF - place_ref[0]
    contributions(
        [first + i for i in range(GROUP)], lambda: (beam_ref[0:1], beam_ref[1:2]),
        foot_ref, lateral_ref, times_ref, amps_ref, u_ref, store,
    )


def merge_kernel(place_ref, near_ref, seam_ref, outer_ref, out_ref):
    first_chip = place_ref[0] < GROUP // 2
    rows = out_ref.shape[1]
    outer = outer_ref[...].astype(f32)
    zero = jnp.zeros_like(outer)
    for t in range(GROUP):
        before = seam_ref[t].astype(f32) if t < HALF else zero
        after = seam_ref[t - 1].astype(f32) if t >= 1 else zero
        if t == 0:
            before = before + outer
        if t == GROUP - 1:
            after = after + outer
        total = (near_ref[t] + jnp.where(first_chip, before, after)).astype(bf16)
        for o in range(out_ref.shape[0] // GROUP):
            out_ref[o * GROUP + t] = total[o * rows : (o + 1) * rows]


def total_kernel(parts_ref, out_ref):
    total = parts_ref[0].astype(f32)
    for i in range(1, parts_ref.shape[0]):
        total = total + parts_ref[i].astype(f32)
    out_ref[...] = total


def vmem():
    return pl.BlockSpec(memory_space=pltpu.VMEM)


def smem():
    return pl.BlockSpec(memory_space=pltpu.SMEM)


def call(kernel, out_shape, in_specs, mib=None, scratch=(), flops=0):
    many = isinstance(out_shape, tuple)
    limit = None if mib is None else mib * 1024 * 1024
    return pl.pallas_call(
        kernel,
        out_shape=out_shape,
        in_specs=in_specs,
        out_specs=tuple(vmem() for _ in out_shape) if many else vmem(),
        scratch_shapes=scratch,
        compiler_params=pltpu.CompilerParams(vmem_limit_bytes=limit),
        cost_estimate=pl.CostEstimate(flops=flops, bytes_accessed=1 << 20, transcendentals=0),
    )


def struct(*shape):
    return jax.ShapeDtypeStruct(shape, bf16)


def struct32(*shape):
    return jax.ShapeDtypeStruct(shape, f32)


def shards(traces, centre_ids, midpoint_bins, ray_times, ray_amps, beam_lateral, footprint):
    slab_axes = ("group", "chip", "core")
    my_slab = lax.axis_index(slab_axes)
    slabs = lax.axis_size(slab_axes)
    offsets = lax.axis_size("offset")
    count = traces.shape[1]
    depth = ray_times.shape[4]
    part = depth // offsets
    high, low = dft_tables()
    routed = call(route_kernel, struct(slabs * ROWS, LANES), [vmem()] * 5)(
        centre_ids.reshape(1, count), midpoint_bins, traces[0], jnp.asarray(high), jnp.asarray(low)
    )
    arrived = lax.all_to_all(
        routed.reshape(slabs, ROWS, LANES), slab_axes, split_axis=0, concat_axis=0, tiled=True
    ).reshape(slabs * ROWS, LANES)

    lateral = lax.dynamic_index_in_dim(beam_lateral[0], my_slab, 0, keepdims=False)
    lateral = jnp.tile(lateral, (1, LANES // P_SIZE))
    foot = lax.dynamic_index_in_dim(footprint, my_slab, 0, keepdims=False)
    u_rows = 2 * P_SIZE * NF
    place = (my_slab % GROUP).astype(jnp.int32).reshape(1)
    cosine, sine, spread = slant_tables()
    to_seam, to_outer, beams = call(
        lambda *refs: far_kernel(*refs, scale=1.0 / math.sqrt(NT * count)),
        (struct(HALF, depth, XW), struct(depth, XW), struct32(2, NF * P_SIZE)),
        [smem()] * 2 + [vmem()] * 7,
        24,
        [pltpu.VMEM((HALF, u_rows, depth), bf16)],
    )(
        place, foot, arrived, lateral, ray_times[0, 0], ray_amps[0, 0],
        jnp.asarray(spread), jnp.asarray(cosine), jnp.asarray(sine),
    )

    seam_step = (-2, -2, 2, 2)
    outer_step = (0, 3, -3, 0)
    over_seam = [(i, i + seam_step[i % GROUP]) for i in range(slabs)]
    outward = [(i, i + outer_step[i % GROUP]) for i in range(slabs)]
    over_seam = [(i, j) for i, j in over_seam if 0 <= j < slabs]
    outward = [(i, j) for i, j in outward if 0 <= j < slabs and i != j]
    from_seam = lax.ppermute(to_seam, slab_axes, over_seam)
    from_outer = lax.ppermute(to_outer, slab_axes, outward)
    near = call(
        near_kernel,
        struct32(GROUP, depth, XW),
        [smem()] * 2 + [vmem()] * 4,
        24,
        [pltpu.VMEM((GROUP, u_rows, depth), bf16)],
        flops=1 << 28,
    )(place, foot, beams, lateral, ray_times[0, 0], ray_amps[0, 0])
    merged = call(merge_kernel, struct(GROUP * offsets, part, XW), [smem()] + [vmem()] * 3, 8)(
        place, near, from_seam, from_outer
    )
    parts = lax.all_to_all(
        merged, ("offset", "chip", "core"), split_axis=0, concat_axis=0, tiled=True
    )
    return call(total_kernel, struct32(part, XW), [vmem()], 4)(parts)


def solution(mesh):
    offsets, slabs = mesh.devices.shape
    shape = (offsets, slabs // GROUP, GROUP // 2, 2)
    chips = Mesh(mesh.devices.reshape(shape), ("offset", "group", "chip", "core"))
    slab = ("group", "chip", "core")
    return jax.shard_map(
        shards,
        mesh=chips,
        in_specs=(
            P("offset", slab, None),
            P("offset", slab, None),
            P("offset", slab),
            P("offset", slab, None, None, None),
            P("offset", slab, None, None, None),
            P("offset", None, None, None),
            P(),
        ),
        out_specs=P("offset", slab),
        check_vma=False,
    )
```

```python
import math

import jax
import jax.numpy as jnp
import numpy as np
from jax import lax
from jax.experimental import pallas as pl
from jax.experimental.pallas import tpu as pltpu
from jax.sharding import Mesh
from jax.sharding import PartitionSpec as P

NT = 256
NF = 64
KLO = 8
P_SIZE = 16
BINS = 16
CAP = 6
WIN = 7
XW = 128
ROWS = 8
LANES = 128
HALF = (WIN - 1) // 2
GROUPS = P_SIZE * NF // LANES
GROUP = 4

two_pi = 2.0 * math.pi
slow_step = 0.25
width_scale = 200.0
omega_step = two_pi / NT

f32 = jnp.float32
bf16 = jnp.bfloat16


def dft_tables():
    sample = np.arange(NT)[:, None]
    turns = (sample * (np.arange(NF)[None, :] + KLO) % NT) * (two_pi / NT)
    table = np.concatenate([np.cos(turns), -np.sin(turns)], axis=1).astype(np.float32)
    high = table.astype(bf16)
    low = (table - high.astype(np.float32)).astype(bf16)
    return high, low


def slant_tables():
    freq = (np.arange(NF) + KLO) * omega_step
    slow = (np.arange(P_SIZE) - (P_SIZE - 1) / 2.0) * slow_step
    place = np.arange(BINS) - (BINS - 1) / 2.0
    phase = place[:, None, None] * freq[None, :, None] * slow[None, None, :]
    phase = phase.reshape(BINS, NF * P_SIZE)
    spread = np.arange(2 * NF)[:, None] % NF == np.arange(NF * P_SIZE)[None, :] // P_SIZE
    return (
        np.cos(phase).astype(np.float32),
        np.sin(phase).astype(np.float32),
        spread.astype(np.float32).astype(bf16),
    )


def iota(shape, dim):
    return lax.broadcasted_iota(jnp.int32, shape, dim)


def dot(a, b):
    return jnp.dot(a, b, preferred_element_type=f32)


def route_kernel(ids_ref, bins_ref, traces_ref, high_ref, low_ref, out_ref):
    count = traces_ref.shape[0]
    square = (count, count)
    row, col = iota(square, 0), iota(square, 1)
    ids_across = ids_ref[...]
    ids_down = jnp.sum(
        jnp.where(row == col, ids_across.astype(f32), 0.0), axis=1, keepdims=True
    )
    same = ids_down == ids_across.astype(f32)
    rank_across = jnp.sum(jnp.where(same & (row < col), 1.0, 0.0), axis=0, keepdims=True)
    rank_down = jnp.sum(jnp.where(same & (col < row), 1.0, 0.0), axis=1, keepdims=True)
    place_across = bins_ref[...].astype(f32) - (BINS - 1) / 2.0
    place_down = jnp.sum(jnp.where(row == col, place_across, 0.0), axis=1, keepdims=True)
    traces = traces_ref[...]
    spectrum = dot(traces, high_ref[...]) + dot(traces, low_ref[...])
    places = jnp.where(col == rank_down.astype(jnp.int32), place_down, 0.0)
    values = jnp.concatenate([spectrum, places], axis=1).astype(bf16)
    out_rows = out_ref.shape[0]
    slot = iota((out_rows, count), 0)
    place_row = slot % ROWS == CAP
    target = ids_across * ROWS + rank_across.astype(jnp.int32)
    pick = (slot == target) | (place_row & (slot // ROWS == ids_across))
    picked = dot(jnp.where(pick, 1.0, 0.0).astype(bf16), values)
    out_ref[...] = jnp.where(place_row, picked[:, LANES:], picked[:, :LANES]).astype(bf16)


def slant_stack(arrived, spread, cosine, sine, scale):
    rows = arrived.shape[0]
    full = arrived.astype(f32).reshape(rows // ROWS, ROWS, LANES)
    sub, lane = iota((rows // ROWS, ROWS, LANES), 1), iota((rows // ROWS, ROWS, LANES), 2)
    own = jnp.where(sub == lane, jnp.broadcast_to(full[:, CAP : CAP + 1, :], full.shape), 0.0)
    own = own.reshape(rows, LANES).astype(bf16)
    place = dot(own, jnp.ones((LANES, LANES), bf16))
    bin_place = iota((rows, LANES), 1).astype(f32) - (BINS - 1) / 2.0
    in_bin = jnp.where((place == bin_place) & (place != 0.0), 1.0, 0.0).astype(bf16)
    binned = lax.dot_general(
        in_bin, arrived, (((0,), (0,)), ((), ())), preferred_element_type=f32
    )[:BINS]
    real = iota((BINS, LANES), 1) < NF
    binned_re = jnp.where(real, binned, 0.0)
    binned_im = jnp.where(real, 0.0, binned)
    parts = []
    for part in (binned_re, binned_im):
        high = part.astype(bf16)
        parts += [high, (part - high.astype(f32)).astype(bf16)]
    wide = dot(jnp.concatenate(parts, axis=0), spread)
    wide_re = wide[:BINS] + wide[BINS : 2 * BINS]
    wide_im = wide[2 * BINS : 3 * BINS] + wide[3 * BINS :]
    beam_re = jnp.sum(wide_re * cosine + wide_im * sine, axis=0, keepdims=True)
    beam_im = jnp.sum(wide_im * cosine - wide_re * sine, axis=0, keepdims=True)
    return (
        (beam_re * scale).astype(bf16).astype(f32),
        (beam_im * scale).astype(bf16).astype(f32),
    )


def cos_sin_turns(turns):
    half = (turns - 0.5) * math.pi
    sq = half * half
    sin_of = 1.0 / 6227020800.0
    for divisor in (-39916800.0, 362880.0, -5040.0, 120.0, -6.0, 1.0):
        sin_of = sin_of * sq + 1.0 / divisor
    sin_of = sin_of * half
    cos_of = 1.0 / 479001600.0
    for divisor in (-3628800.0, 40320.0, -720.0, 24.0, -2.0, 1.0):
        cos_of = cos_of * sq + 1.0 / divisor
    return 2.0 * sin_of * sin_of - 1.0, -2.0 * sin_of * cos_of


def u_groups(u_ref, times, amps):
    def times_of(a, b):
        return a[0] * b[0] - a[1] * b[1], a[0] * b[1] + a[1] * b[0]

    one = cos_sin_turns(times * (1.0 / NT))
    two = times_of(one, one)
    four = times_of(two, two)
    eight = times_of(four, four)
    start = (amps * eight[0], amps * eight[1])
    walk = [start, times_of(start, one), times_of(start, two)]
    walk.append(times_of(walk[1], two))
    values = [(c, -s) for c, s in walk]
    factor = 2.0 * two[0]
    for j in range(NF):
        if j >= 4:
            values.append(
                tuple(factor * values[j - 2][i] - values[j - 4][i] for i in range(2))
            )
        group, inner = divmod(j, LANES // P_SIZE)
        for i in range(2):
            first = group * 2 * LANES + i * LANES + inner * P_SIZE
            u_ref[pl.ds(first, P_SIZE), :] = values[j][i].astype(bf16)
        if inner == LANES // P_SIZE - 1:
            yield


def v_groups(lateral, first, end, beam_re, beam_im):
    xs = iota((XW, LANES), 0).astype(f32)
    freq = (iota((XW, LANES), 1) // P_SIZE + KLO).astype(f32) * (omega_step / width_scale)
    away = xs - lateral
    minus = -(away * away)
    inside = (xs >= first) & (xs < end)
    gauss = jnp.where(inside, jnp.exp(minus * freq), 0.0) * (1.0 / math.sqrt(P_SIZE * NF))
    ratio = jnp.exp(minus * ((LANES // P_SIZE) * omega_step / width_scale))
    for group in range(GROUPS):
        lanes = slice(group * LANES, (group + 1) * LANES)
        yield jnp.concatenate(
            [(gauss * beam_re[:, lanes]).astype(bf16), (gauss * beam_im[:, lanes]).astype(bf16)],
            axis=1,
        )
        gauss = gauss * ratio


def contributions(windows, u_ref):
    blocks = []
    for _ in u_groups(u_ref.at[0], *windows[0][:2]):
        pass
    for i, window in enumerate(windows):
        following = iter(())
        if i + 1 < len(windows):
            following = u_groups(u_ref.at[i + 1], *windows[i + 1][:2])
        total = None
        for group, v in enumerate(v_groups(*window[2:])):
            part = dot(v, u_ref[i, pl.ds(group * 2 * LANES, 2 * LANES), :])
            total = part if total is None else total + part
            next(following, None)
        blocks.append(total.T)
    return blocks


def pack_kernel(place_ref, foot_ref, lateral_ref, times_ref, amps_ref, seam_ref, outer_ref):
    place = place_ref[0]

    def pack(w, ref):
        ref[0:P_SIZE] = times_ref[w]
        ref[P_SIZE : 2 * P_SIZE] = amps_ref[w]
        sub = iota((8, LANES), 0)
        first, end = foot_ref[w, 0].astype(f32), foot_ref[w, 1].astype(f32)
        lateral = jnp.broadcast_to(lateral_ref[pl.ds(w, 1), :], (8, LANES))
        tail = jnp.where(sub == 0, lateral, jnp.where(sub == 1, first, end))
        ref[2 * P_SIZE :] = jnp.concatenate([tail] * (ref.shape[1] // LANES), axis=1)

    for i in range(HALF):
        pack((i - place + WIN) % WIN, seam_ref.at[i])
    pack(jnp.where(place == 1, WIN - 1, 0), outer_ref)


def beams_kernel(arrived_ref, spread_ref, cos_ref, sin_ref, beam_ref, *, scale):
    beams = slant_stack(arrived_ref[...], spread_ref[...], cos_ref[...], sin_ref[...], scale)
    for i in range(2):
        beam_ref[i : i + 1] = beams[i]


def near_kernel(
    place_ref, foot_ref, beam_ref, lateral_ref, times_ref, amps_ref, near_ref, u_ref
):
    windows = []
    for i in range(GROUP):
        w = HALF - place_ref[0] + i
        first, end = foot_ref[w, 0].astype(f32), foot_ref[w, 1].astype(f32)
        windows.append(
            (times_ref[w], amps_ref[w], lateral_ref[pl.ds(w, 1), :], first, end,
             beam_ref[0:1], beam_ref[1:2])
        )
    for i, block in enumerate(contributions(windows, u_ref)):
        near_ref[i] = block


def far_kernel(
    place_ref, near_ref, seam_beam_ref, outer_beam_ref, seam_ref, outer_ref, out_ref, u_ref
):
    place = place_ref[0]
    rows = out_ref.shape[1]
    windows = []
    for i in range(HALF):
        rays, beam_re, beam_im = seam_ref[i], seam_beam_ref[0:1], seam_beam_ref[1:2]
        if i != 1:
            from_outer = place == (0 if i else GROUP - 1)
            rays = jnp.where(from_outer, outer_ref[...], rays)
            beam_re = jnp.where(from_outer, outer_beam_ref[0:1], beam_re)
            beam_im = jnp.where(from_outer, outer_beam_ref[1:2], beam_im)
        tail = rays[2 * P_SIZE :, :LANES]
        windows.append(
            (rays[:P_SIZE], rays[P_SIZE : 2 * P_SIZE], tail[0:1], tail[1:2], tail[2:3],
             beam_re, beam_im)
        )
    blocks = contributions(windows, u_ref)
    first_chip = place < GROUP // 2
    zero = jnp.zeros_like(blocks[0])
    takes = (
        ((first_chip, 0), (place == 0, 2)),
        ((first_chip, 1), (place == 2, 0)),
        ((place == 1, 2), (~first_chip, 1)),
        ((place == 3, 0), (~first_chip, 2)),
    )
    for t, taken in enumerate(takes):
        total = near_ref[t]
        for when, i in taken:
            total = total + jnp.where(when, blocks[i], zero)
        total = total.astype(bf16)
        for o in range(out_ref.shape[0] // GROUP):
            out_ref[o * GROUP + t] = total[o * rows : (o + 1) * rows]


def total_kernel(parts_ref, out_ref):
    total = parts_ref[0].astype(f32)
    for i in range(1, parts_ref.shape[0]):
        total = total + parts_ref[i].astype(f32)
    out_ref[...] = total


def vmem():
    return pl.BlockSpec(memory_space=pltpu.VMEM)


def smem():
    return pl.BlockSpec(memory_space=pltpu.SMEM)


def call(kernel, out_shape, in_specs, mib=None, scratch=(), flops=0):
    many = isinstance(out_shape, tuple)
    limit = None if mib is None else mib * 1024 * 1024
    return pl.pallas_call(
        kernel,
        out_shape=out_shape,
        in_specs=in_specs,
        out_specs=tuple(vmem() for _ in out_shape) if many else vmem(),
        scratch_shapes=scratch,
        compiler_params=pltpu.CompilerParams(vmem_limit_bytes=limit),
        cost_estimate=pl.CostEstimate(flops=flops, bytes_accessed=1 << 20, transcendentals=0),
    )


def struct(*shape):
    return jax.ShapeDtypeStruct(shape, bf16)


def struct32(*shape):
    return jax.ShapeDtypeStruct(shape, f32)


def shards(traces, centre_ids, midpoint_bins, ray_times, ray_amps, beam_lateral, footprint):
    slab_axes = ("group", "chip", "core")
    my_slab = lax.axis_index(slab_axes)
    slabs = lax.axis_size(slab_axes)
    offsets = lax.axis_size("offset")
    count = traces.shape[1]
    depth = ray_times.shape[4]
    part = depth // offsets
    high, low = dft_tables()
    routed = call(route_kernel, struct(slabs * ROWS, LANES), [vmem()] * 5)(
        centre_ids.reshape(1, count), midpoint_bins, traces[0], jnp.asarray(high), jnp.asarray(low)
    )
    arrived = lax.all_to_all(
        routed.reshape(slabs, ROWS, LANES), slab_axes, split_axis=0, concat_axis=0, tiled=True
    ).reshape(slabs * ROWS, LANES)

    lateral = lax.dynamic_index_in_dim(beam_lateral[0], my_slab, 0, keepdims=False)
    lateral = jnp.tile(lateral, (1, LANES // P_SIZE))
    foot = lax.dynamic_index_in_dim(footprint, my_slab, 0, keepdims=False)
    u_rows = 2 * P_SIZE * NF
    place = (my_slab % GROUP).astype(jnp.int32).reshape(1)

    seam_step = (-2, -2, 2, 2)
    outer_step = (0, 3, -3, 0)
    over_seam = [(i, i + seam_step[i % GROUP]) for i in range(slabs)]
    outward = [(i, i + outer_step[i % GROUP]) for i in range(slabs)]
    over_seam = [(i, j) for i, j in over_seam if 0 <= j < slabs]
    outward = [(i, j) for i, j in outward if 0 <= j < slabs and i != j]
    ray_rows = 2 * P_SIZE + 8
    seam_rays, outer_rays = call(
        pack_kernel,
        (struct32(HALF, ray_rows, depth), struct32(ray_rows, depth)),
        [smem()] * 2 + [vmem()] * 3,
        8,
        flops=1 << 28,
    )(place, foot, lateral, ray_times[0, 0], ray_amps[0, 0])
    seam_rays = lax.ppermute(seam_rays, slab_axes, over_seam)
    outer_rays = lax.ppermute(outer_rays, slab_axes, outward)

    cosine, sine, spread = slant_tables()
    beams = call(
        lambda *refs: beams_kernel(*refs, scale=1.0 / math.sqrt(NT * count)),
        struct32(2, NF * P_SIZE),
        [vmem()] * 4,
        8,
    )(arrived, jnp.asarray(spread), jnp.asarray(cosine), jnp.asarray(sine))
    seam_beams = lax.ppermute(beams, slab_axes, over_seam)
    outer_beams = lax.ppermute(beams, slab_axes, outward)
    near = call(
        near_kernel,
        struct32(GROUP, depth, XW),
        [smem()] * 2 + [vmem()] * 4,
        24,
        [pltpu.VMEM((GROUP, u_rows, depth), bf16)],
        flops=1 << 28,
    )(place, foot, beams, lateral, ray_times[0, 0], ray_amps[0, 0])
    merged = call(
        far_kernel,
        struct(GROUP * offsets, part, XW),
        [smem()] + [vmem()] * 5,
        24,
        [pltpu.VMEM((HALF, u_rows, depth), bf16)],
    )(place, near, seam_beams, outer_beams, seam_rays, outer_rays)
    parts = lax.all_to_all(
        merged, ("offset", "chip", "core"), split_axis=0, concat_axis=0, tiled=True
    )
    return call(total_kernel, struct32(part, XW), [vmem()], 4)(parts)


def solution(mesh):
    offsets, slabs = mesh.devices.shape
    shape = (offsets, slabs // GROUP, GROUP // 2, 2)
    chips = Mesh(mesh.devices.reshape(shape), ("offset", "group", "chip", "core"))
    slab = ("group", "chip", "core")
    return jax.shard_map(
        shards,
        mesh=chips,
        in_specs=(
            P("offset", slab, None),
            P("offset", slab, None),
            P("offset", slab),
            P("offset", slab, None, None, None),
            P("offset", slab, None, None, None),
            P("offset", None, None, None),
            P(),
        ),
        out_specs=P("offset", slab),
        check_vma=False,
    )
```

```python
import functools
import math

import jax
import jax.numpy as jnp
import numpy as np
from jax import lax
from jax.experimental import pallas as pl
from jax.experimental.pallas import tpu as pltpu
from jax.sharding import Mesh
from jax.sharding import PartitionSpec as P

NT = 256
NF = 64
KLO = 8
P_SIZE = 16
BINS = 16
CAP = 6
WIN = 7
XW = 128
ROWS = 16
LANES = 128
HALF = (WIN - 1) // 2
GROUPS = P_SIZE * NF // LANES
GROUP = 4
FIRST_SLAB = 16
SECOND_STEP = (-1, -3, 3, 1)
THIRD_STEP = (-3, -4, 4, 3)
THIRD_SLOT = (0, 3, 3, 0)

two_pi = 2.0 * math.pi
slow_step = 0.25
width_scale = 200.0
omega_step = two_pi / NT

f32 = jnp.float32
bf16 = jnp.bfloat16


def dft_tables():
    sample = np.arange(NT)[:, None]
    turns = (sample * (np.arange(NF)[None, :] + KLO) % NT) * (two_pi / NT)
    table = np.concatenate([np.cos(turns), -np.sin(turns)], axis=1).astype(np.float32)
    high = table.astype(bf16)
    low = (table - high.astype(np.float32)).astype(bf16)
    return high, low


def slant_tables():
    freq = (np.arange(NF) + KLO) * omega_step
    slow = (np.arange(P_SIZE) - (P_SIZE - 1) / 2.0) * slow_step
    place = np.arange(BINS) - (BINS - 1) / 2.0
    phase = place[:, None, None] * freq[None, :, None] * slow[None, None, :]
    phase = phase.reshape(BINS, NF * P_SIZE)
    spread = np.arange(2 * NF)[:, None] % NF == np.arange(NF * P_SIZE)[None, :] // P_SIZE
    return (
        np.cos(phase).astype(np.float32),
        np.sin(phase).astype(np.float32),
        spread.astype(np.float32).astype(bf16),
    )


def iota(shape, dim):
    return lax.broadcasted_iota(jnp.int32, shape, dim)


def dot(a, b):
    return jnp.dot(a, b, preferred_element_type=f32)


def by_place(place, choices):
    value = choices[-1]
    for i in reversed(range(len(choices) - 1)):
        value = jnp.where(place == i, choices[i], value)
    return value


def route_kernel(ids_ref, bins_ref, traces_ref, high_ref, low_ref, out_ref, *, groups):
    count = traces_ref.shape[0]
    square = (count, count)
    row, col = iota(square, 0), iota(square, 1)
    ids_across = ids_ref[...]
    ids_down = jnp.sum(
        jnp.where(row == col, ids_across.astype(f32), 0.0), axis=1, keepdims=True
    )
    same = ids_down == ids_across.astype(f32)
    rank_across = jnp.sum(jnp.where(same & (row < col), 1.0, 0.0), axis=0, keepdims=True)
    code_across = ids_across * 8 + rank_across.astype(jnp.int32)
    place_across = bins_ref[...].astype(f32) - (BINS - 1) / 2.0
    place_down = jnp.sum(jnp.where(row == col, place_across, 0.0), axis=1, keepdims=True)
    traces = traces_ref[...]
    spectrum = dot(traces, high_ref[...]) + dot(traces, low_ref[...])
    values = jnp.concatenate([spectrum, jnp.broadcast_to(place_down, square)], axis=1).astype(bf16)

    group_rows = GROUP * ROWS
    slot = iota((group_rows, count), 0) % ROWS
    slab = iota((group_rows, count), 0) // ROWS
    second = (slab + by_place(slab, SECOND_STEP)) * 8 + slot - CAP
    third = (slab + by_place(slab, THIRD_STEP)) * 8 + slot - 2 * CAP
    third = third + by_place(slab, THIRD_SLOT)
    wanted = jnp.where(slot < CAP, slab * 8 + slot, jnp.where(slot < 2 * CAP, second, third))
    wanted = jnp.where(slot == ROWS - 1, -(1 << 20), wanted)
    pick = [
        jnp.where(wanted + group * GROUP * 8 == code_across, 1.0, 0.0).astype(bf16)
        for group in groups
    ]
    picked = dot(jnp.concatenate(pick, axis=0), values).reshape(-1, ROWS, 2 * LANES)
    shape = picked.shape[:2] + (LANES,)
    places = jnp.where(iota(shape, 1) == iota(shape, 2), picked[:, :, LANES:], 0.0)
    places = jnp.broadcast_to(jnp.sum(places, axis=1, keepdims=True), shape)
    block = jnp.where(iota(shape, 1) == ROWS - 1, places, picked[:, :, :LANES])
    out_ref[...] = block.reshape(out_ref.shape).astype(bf16)


def slant_stack(arrived, spread, cosine, sine, scale):
    rows = arrived.shape[0]
    shape = (rows // ROWS, ROWS, LANES)
    full = arrived.astype(f32).reshape(shape)
    last = jnp.broadcast_to(full[:, ROWS - 1 :, :], shape)
    own = jnp.where(iota(shape, 1) == iota(shape, 2), last, 0.0).reshape(rows, LANES).astype(bf16)
    place = dot(own, jnp.ones((LANES, LANES), bf16))
    lane, slot = iota((rows, LANES), 1), iota((rows, LANES), 0) % ROWS
    centre = jnp.where(slot < CAP, 0, jnp.where(slot < 2 * CAP, 1, 2))
    bin_place = (lane % BINS).astype(f32) - (BINS - 1) / 2.0
    hit = (place == bin_place) & (lane // BINS == centre) & (slot < ROWS - 1)
    in_bin = jnp.where(hit, 1.0, 0.0).astype(bf16)
    number = 3 * BINS
    binned = lax.dot_general(
        in_bin, arrived, (((0,), (0,)), ((), ())), preferred_element_type=f32
    )[:number]
    real = iota((number, LANES), 1) < NF
    parts = []
    for part in (jnp.where(real, binned, 0.0), jnp.where(real, 0.0, binned)):
        high = part.astype(bf16)
        parts += [high, (part - high.astype(f32)).astype(bf16)]
    wide = dot(jnp.concatenate(parts, axis=0), spread)
    wide_re = wide[:number] + wide[number : 2 * number]
    wide_im = wide[2 * number : 3 * number] + wide[3 * number :]
    beams = []
    for first in range(0, number, BINS):
        re, im = wide_re[first : first + BINS], wide_im[first : first + BINS]
        beam_re = jnp.sum(re * cosine + im * sine, axis=0, keepdims=True)
        beam_im = jnp.sum(im * cosine - re * sine, axis=0, keepdims=True)
        beams.append(
            (
                (beam_re * scale).astype(bf16).astype(f32),
                (beam_im * scale).astype(bf16).astype(f32),
            )
        )
    return beams


def cos_sin_turns(turns):
    half = (turns - 0.5) * math.pi
    sq = half * half
    sin_of = 1.0 / 6227020800.0
    for divisor in (-39916800.0, 362880.0, -5040.0, 120.0, -6.0, 1.0):
        sin_of = sin_of * sq + 1.0 / divisor
    sin_of = sin_of * half
    cos_of = 1.0 / 479001600.0
    for divisor in (-3628800.0, 40320.0, -720.0, 24.0, -2.0, 1.0):
        cos_of = cos_of * sq + 1.0 / divisor
    return 2.0 * sin_of * sin_of - 1.0, -2.0 * sin_of * cos_of


def u_groups(u_ref, times, amps):
    def times_of(a, b):
        return a[0] * b[0] - a[1] * b[1], a[0] * b[1] + a[1] * b[0]

    one = cos_sin_turns(times * (1.0 / NT))
    two = times_of(one, one)
    four = times_of(two, two)
    eight = times_of(four, four)
    start = (amps * eight[0], amps * eight[1])
    walk = [start, times_of(start, one), times_of(start, two)]
    walk.append(times_of(walk[1], two))
    values = [(c, -s) for c, s in walk]
    factor = 2.0 * two[0]
    for j in range(NF):
        if j >= 4:
            values.append(
                tuple(factor * values[j - 2][i] - values[j - 4][i] for i in range(2))
            )
        group, inner = divmod(j, LANES // P_SIZE)
        for i in range(2):
            first = group * 2 * LANES + i * LANES + inner * P_SIZE
            u_ref[pl.ds(first, P_SIZE), :] = values[j][i].astype(bf16)
        if inner == LANES // P_SIZE - 1:
            yield


def v_groups(lateral, first, end, beam_re, beam_im):
    xs = iota((XW, LANES), 0).astype(f32)
    freq = (iota((XW, LANES), 1) // P_SIZE + KLO).astype(f32) * (omega_step / width_scale)
    away = xs - lateral
    minus = -(away * away)
    inside = (xs >= first) & (xs < end)
    gauss = jnp.where(inside, jnp.exp(minus * freq), 0.0) * (1.0 / math.sqrt(P_SIZE * NF))
    ratio = jnp.exp(minus * ((LANES // P_SIZE) * omega_step / width_scale))
    for group in range(GROUPS):
        lanes = slice(group * LANES, (group + 1) * LANES)
        yield jnp.concatenate(
            [(gauss * beam_re[:, lanes]).astype(bf16), (gauss * beam_im[:, lanes]).astype(bf16)],
            axis=1,
        )
        gauss = gauss * ratio


def contributions(windows, u_ref):
    blocks = []
    for _ in u_groups(u_ref.at[0], *windows[0][:2]):
        pass
    for i, window in enumerate(windows):
        following = iter(())
        if i + 1 < len(windows):
            following = u_groups(u_ref.at[i + 1], *windows[i + 1][:2])
        total = None
        for group, v in enumerate(v_groups(*window[2:])):
            part = dot(v, u_ref[i, pl.ds(group * 2 * LANES, 2 * LANES), :])
            total = part if total is None else total + part
            next(following, None)
        blocks.append(total)
    return blocks


def pack_kernel(
    place_ref, foot_ref, lateral_ref, times_ref, amps_ref, seam_ref, outer_ref, near_ref, flag_ref
):
    place = place_ref[0]

    def pack(w, ref):
        ref[0:P_SIZE] = times_ref[w]
        ref[P_SIZE : 2 * P_SIZE] = amps_ref[w]
        sub = iota((8, LANES), 0)
        first, end = foot_ref[w, 0].astype(f32), foot_ref[w, 1].astype(f32)
        lateral = jnp.broadcast_to(lateral_ref[pl.ds(w, 1), :], (8, LANES))
        tail = jnp.where(sub == 0, lateral, jnp.where(sub == 1, first, end))
        ref[2 * P_SIZE :] = jnp.concatenate([tail] * (ref.shape[1] // LANES), axis=1)

    base = jnp.where(place < GROUP // 2, 0, WIN - place)
    for i in range(HALF):
        pack(jnp.minimum(base + i, WIN - 1), seam_ref.at[i])
    pack(jnp.where(place == 1, WIN - 1, 0), outer_ref)
    for i in range(GROUP):
        pack(HALF - place + i, near_ref.at[i])
    flag_ref[...] = jnp.full(flag_ref.shape, place.astype(f32))


def unpack(rays):
    tail = rays[2 * P_SIZE :, :LANES]
    return rays[:P_SIZE], rays[P_SIZE : 2 * P_SIZE], tail[0:1], tail[1:2], tail[2:3]


def migrate_kernel(
    flag_ref, arrived_ref, spread_ref, cos_ref, sin_ref, near_ref, second_ref, third_0_ref,
    third_1_ref, out_ref, u_ref, *, scale,
):
    own, second, third = slant_stack(
        arrived_ref[...], spread_ref[...], cos_ref[...], sin_ref[...], scale
    )
    windows = [unpack(near_ref[i]) + own for i in range(GROUP)]
    windows += [unpack(second_ref[i]) + second for i in range(HALF)]
    windows += [unpack(third_0_ref[...] + third_1_ref[...]) + third]
    blocks = contributions(windows, u_ref)
    near, (a, b, c, d) = blocks[:GROUP], blocks[GROUP:]
    rows = out_ref.shape[1]
    place = flag_ref[0:1, :]
    is_0, is_2, is_3 = place == 0.0, place == 2.0, place == 3.0
    first = place < GROUP / 2

    def when(condition, block):
        return jnp.where(condition, block, 0.0)

    totals = (
        near[0] + when(first, a + d),
        near[1] + when(first, b) + when(is_3, a),
        near[2] + when(is_0, c) + when(is_3, b) + when(is_2, a),
        near[3] + when(is_3, c) + when(is_2, b) + when(~first, d),
    )
    for t, total in enumerate(totals):
        total = total.T.astype(bf16)
        for o in range(out_ref.shape[0] // GROUP):
            out_ref[o * GROUP + t] = total[o * rows : (o + 1) * rows]


def total_kernel(parts_ref, out_ref):
    total = parts_ref[0].astype(f32)
    for i in range(1, parts_ref.shape[0]):
        total = total + parts_ref[i].astype(f32)
    out_ref[...] = total


def vmem():
    return pl.BlockSpec(memory_space=pltpu.VMEM)


def smem():
    return pl.BlockSpec(memory_space=pltpu.SMEM)


def call(kernel, out_shape, in_specs, mib=None, scratch=(), flops=0):
    many = isinstance(out_shape, tuple)
    limit = None if mib is None else mib * 1024 * 1024
    return pl.pallas_call(
        kernel,
        out_shape=out_shape,
        in_specs=in_specs,
        out_specs=tuple(vmem() for _ in out_shape) if many else vmem(),
        scratch_shapes=scratch,
        compiler_params=pltpu.CompilerParams(vmem_limit_bytes=limit),
        cost_estimate=pl.CostEstimate(flops=flops, bytes_accessed=1 << 20, transcendentals=0),
    )


def struct(*shape):
    return jax.ShapeDtypeStruct(shape, bf16)


def struct32(*shape):
    return jax.ShapeDtypeStruct(shape, f32)


def shards(traces, centre_ids, midpoint_bins, ray_times, ray_amps, beam_lateral, footprint):
    slab_axes = ("group", "chip", "core")
    my_slab = lax.axis_index(slab_axes)
    slabs = lax.axis_size(slab_axes)
    offsets = lax.axis_size("offset")
    count = traces.shape[1]
    depth = ray_times.shape[4]
    part = depth // offsets
    high, low = dft_tables()
    groups = [(FIRST_SLAB // GROUP + i) % (slabs // GROUP) for i in range(slabs // GROUP)]
    order = [group * GROUP + i for group in groups for i in range(GROUP)]
    routed = call(functools.partial(route_kernel, groups=groups), struct(slabs * ROWS, LANES), [vmem()] * 5)(
        centre_ids.reshape(1, count), midpoint_bins, traces[0], jnp.asarray(high), jnp.asarray(low)
    )
    arrived = lax.all_to_all(
        routed.reshape(slabs, ROWS, LANES), slab_axes, split_axis=0, concat_axis=0,
        axis_index_groups=[order], tiled=True,
    ).reshape(slabs * ROWS, LANES)

    lateral = lax.dynamic_index_in_dim(beam_lateral[0], my_slab, 0, keepdims=False)
    lateral = jnp.tile(lateral, (1, LANES // P_SIZE))
    foot = lax.dynamic_index_in_dim(footprint, my_slab, 0, keepdims=False)
    u_rows = 2 * P_SIZE * NF
    place = (my_slab % GROUP).astype(jnp.int32).reshape(1)

    def to_those(steps):
        pairs = [(i + steps[i % GROUP], i) for i in range(slabs) if steps[i % GROUP]]
        return [(i, j) for i, j in pairs if 0 <= i < slabs]

    ray_rows = 2 * P_SIZE + 8
    seam_rays, outer_rays, near_rays, flags = call(
        pack_kernel,
        (
            struct32(HALF, ray_rows, depth), struct32(ray_rows, depth),
            struct32(GROUP, ray_rows, depth), struct32(8, depth),
        ),
        [smem()] * 2 + [vmem()] * 3,
        8,
        flops=1 << 28,
    )(place, foot, lateral, ray_times[0, 0], ray_amps[0, 0])
    second_rays = lax.ppermute(seam_rays, slab_axes, to_those(SECOND_STEP))
    third_0 = lax.ppermute(outer_rays, slab_axes, to_those((THIRD_STEP[0], 0, 0, THIRD_STEP[3])))
    third_1 = lax.ppermute(outer_rays, slab_axes, to_those((0, THIRD_STEP[1], THIRD_STEP[2], 0)))

    cosine, sine, spread = slant_tables()
    merged = call(
        lambda *refs: migrate_kernel(*refs, scale=1.0 / math.sqrt(NT * count)),
        struct(GROUP * offsets, part, XW),
        [vmem()] * 9,
        32,
        [pltpu.VMEM((GROUP + HALF + 1, u_rows, depth), bf16)],
    )(
        flags, arrived, jnp.asarray(spread), jnp.asarray(cosine), jnp.asarray(sine),
        near_rays, second_rays, third_0, third_1,
    )
    parts = lax.all_to_all(
        merged, ("offset", "chip", "core"), split_axis=0, concat_axis=0, tiled=True
    )
    return call(total_kernel, struct32(part, XW), [vmem()], 4)(parts)


def solution(mesh):
    offsets, slabs = mesh.devices.shape
    shape = (offsets, slabs // GROUP, GROUP // 2, 2)
    chips = Mesh(mesh.devices.reshape(shape), ("offset", "group", "chip", "core"))
    slab = ("group", "chip", "core")
    return jax.shard_map(
        shards,
        mesh=chips,
        in_specs=(
            P("offset", slab, None),
            P("offset", slab, None),
            P("offset", slab),
            P("offset", slab, None, None, None),
            P("offset", slab, None, None, None),
            P("offset", None, None, None),
            P(),
        ),
        out_specs=P("offset", slab),
        check_vma=False,
    )
```

```python
import functools
import math

import jax
import jax.numpy as jnp
import numpy as np
from jax import lax
from jax.experimental import pallas as pl
from jax.experimental.pallas import tpu as pltpu
from jax.sharding import Mesh
from jax.sharding import PartitionSpec as P

NT = 256
NF = 64
KLO = 8
P_SIZE = 16
BINS = 16
CAP = 6
WIN = 7
XW = 128
ROWS = 16
LANES = 128
HALF = (WIN - 1) // 2
GROUPS = P_SIZE * NF // LANES
GROUP = 4
FIRST_SLAB = 52
FIRST_OFFSET = 6
SECOND_STEP = (-1, -3, 3, 1)
THIRD_STEP = (-3, -4, 4, 3)
THIRD_SLOT = (0, 3, 3, 0)

two_pi = 2.0 * math.pi
slow_step = 0.25
width_scale = 200.0
omega_step = two_pi / NT

f32 = jnp.float32
bf16 = jnp.bfloat16


def dft_tables():
    sample = np.arange(NT)[:, None]
    turns = (sample * (np.arange(NF)[None, :] + KLO) % NT) * (two_pi / NT)
    table = np.concatenate([np.cos(turns), -np.sin(turns)], axis=1).astype(np.float32)
    high = table.astype(bf16)
    low = (table - high.astype(np.float32)).astype(bf16)
    return high, low


def slant_tables():
    freq = (np.arange(NF) + KLO) * omega_step
    slow = (np.arange(P_SIZE) - (P_SIZE - 1) / 2.0) * slow_step
    place = np.arange(BINS) - (BINS - 1) / 2.0
    phase = place[:, None, None] * freq[None, :, None] * slow[None, None, :]
    phase = phase.reshape(BINS, NF * P_SIZE)
    spread = np.arange(2 * NF)[:, None] % NF == np.arange(NF * P_SIZE)[None, :] // P_SIZE
    return (
        np.cos(phase).astype(np.float32),
        np.sin(phase).astype(np.float32),
        spread.astype(np.float32).astype(bf16),
    )


def iota(shape, dim):
    return lax.broadcasted_iota(jnp.int32, shape, dim)


def dot(a, b):
    return jnp.dot(a, b, preferred_element_type=f32)


def by_place(place, choices):
    value = choices[-1]
    for i in reversed(range(len(choices) - 1)):
        value = jnp.where(place == i, choices[i], value)
    return value


def route_kernel(ids_ref, bins_ref, traces_ref, high_ref, low_ref, out_ref, *, groups):
    count = traces_ref.shape[0]
    square = (count, count)
    row, col = iota(square, 0), iota(square, 1)
    ids_across = ids_ref[...]
    ids_down = jnp.sum(
        jnp.where(row == col, ids_across.astype(f32), 0.0), axis=1, keepdims=True
    )
    same = ids_down == ids_across.astype(f32)
    rank_across = jnp.sum(jnp.where(same & (row < col), 1.0, 0.0), axis=0, keepdims=True)
    code_across = ids_across * 8 + rank_across.astype(jnp.int32)
    place_across = bins_ref[...].astype(f32) - (BINS - 1) / 2.0
    place_down = jnp.sum(jnp.where(row == col, place_across, 0.0), axis=1, keepdims=True)
    traces = traces_ref[...]
    spectrum = dot(traces, high_ref[...]) + dot(traces, low_ref[...])
    values = jnp.concatenate([spectrum, jnp.broadcast_to(place_down, square)], axis=1).astype(bf16)

    group_rows = GROUP * ROWS
    slot = iota((group_rows, count), 0) % ROWS
    slab = iota((group_rows, count), 0) // ROWS
    second = (slab + by_place(slab, SECOND_STEP)) * 8 + slot - CAP
    third = (slab + by_place(slab, THIRD_STEP)) * 8 + slot - 2 * CAP
    third = third + by_place(slab, THIRD_SLOT)
    wanted = jnp.where(slot < CAP, slab * 8 + slot, jnp.where(slot < 2 * CAP, second, third))
    wanted = jnp.where(slot == ROWS - 1, -(1 << 20), wanted)
    pick = [
        jnp.where(wanted + group * GROUP * 8 == code_across, 1.0, 0.0).astype(bf16)
        for group in groups
    ]
    picked = dot(jnp.concatenate(pick, axis=0), values).reshape(-1, ROWS, 2 * LANES)
    shape = picked.shape[:2] + (LANES,)
    places = jnp.where(iota(shape, 1) == iota(shape, 2), picked[:, :, LANES:], 0.0)
    places = jnp.broadcast_to(jnp.sum(places, axis=1, keepdims=True), shape)
    block = jnp.where(iota(shape, 1) == ROWS - 1, places, picked[:, :, :LANES])
    out_ref[...] = block.reshape(out_ref.shape).astype(bf16)


def slant_stack(arrived, spread, cosine, sine, scale):
    rows = arrived.shape[0]
    shape = (rows // ROWS, ROWS, LANES)
    full = arrived.astype(f32).reshape(shape)
    last = jnp.broadcast_to(full[:, ROWS - 1 :, :], shape)
    own = jnp.where(iota(shape, 1) == iota(shape, 2), last, 0.0).reshape(rows, LANES).astype(bf16)
    place = dot(own, jnp.ones((LANES, LANES), bf16))
    lane, slot = iota((rows, LANES), 1), iota((rows, LANES), 0) % ROWS
    centre = jnp.where(slot < CAP, 0, jnp.where(slot < 2 * CAP, 1, 2))
    bin_place = (lane % BINS).astype(f32) - (BINS - 1) / 2.0
    hit = (place == bin_place) & (lane // BINS == centre) & (slot < ROWS - 1)
    in_bin = jnp.where(hit, 1.0, 0.0).astype(bf16)
    number = 3 * BINS
    binned = lax.dot_general(
        in_bin, arrived, (((0,), (0,)), ((), ())), preferred_element_type=f32
    )[:number]
    real = iota((number, LANES), 1) < NF
    parts = []
    for part in (jnp.where(real, binned, 0.0), jnp.where(real, 0.0, binned)):
        high = part.astype(bf16)
        parts += [high, (part - high.astype(f32)).astype(bf16)]
    wide = dot(jnp.concatenate(parts, axis=0), spread)
    wide_re = wide[:number] + wide[number : 2 * number]
    wide_im = wide[2 * number : 3 * number] + wide[3 * number :]
    beams = []
    for first in range(0, number, BINS):
        re, im = wide_re[first : first + BINS], wide_im[first : first + BINS]
        beam_re = jnp.sum(re * cosine + im * sine, axis=0, keepdims=True)
        beam_im = jnp.sum(im * cosine - re * sine, axis=0, keepdims=True)
        beams.append(
            (
                (beam_re * scale).astype(bf16).astype(f32),
                (beam_im * scale).astype(bf16).astype(f32),
            )
        )
    return beams


def cos_sin_turns(turns):
    half = (turns - 0.5) * math.pi
    sq = half * half
    sin_of = 1.0 / 6227020800.0
    for divisor in (-39916800.0, 362880.0, -5040.0, 120.0, -6.0, 1.0):
        sin_of = sin_of * sq + 1.0 / divisor
    sin_of = sin_of * half
    cos_of = 1.0 / 479001600.0
    for divisor in (-3628800.0, 40320.0, -720.0, 24.0, -2.0, 1.0):
        cos_of = cos_of * sq + 1.0 / divisor
    return 2.0 * sin_of * sin_of - 1.0, -2.0 * sin_of * cos_of


def u_groups(u_ref, times, amps):
    def times_of(a, b):
        return a[0] * b[0] - a[1] * b[1], a[0] * b[1] + a[1] * b[0]

    one = cos_sin_turns(times * (1.0 / NT))
    two = times_of(one, one)
    four = times_of(two, two)
    eight = times_of(four, four)
    start = (amps * eight[0], amps * eight[1])
    walk = [start, times_of(start, one), times_of(start, two)]
    walk.append(times_of(walk[1], two))
    values = [(c, -s) for c, s in walk]
    factor = 2.0 * two[0]
    for j in range(NF):
        if j >= 4:
            values.append(
                tuple(factor * values[j - 2][i] - values[j - 4][i] for i in range(2))
            )
        group, inner = divmod(j, LANES // P_SIZE)
        for i in range(2):
            first = group * 2 * LANES + i * LANES + inner * P_SIZE
            u_ref[pl.ds(first, P_SIZE), :] = values[j][i].astype(bf16)
        if inner == LANES // P_SIZE - 1:
            yield


def v_groups(lateral, first, end, beam_re, beam_im):
    xs = iota((XW, LANES), 0).astype(f32)
    freq = (iota((XW, LANES), 1) // P_SIZE + KLO).astype(f32) * (omega_step / width_scale)
    away = xs - lateral
    minus = -(away * away)
    inside = (xs >= first) & (xs < end)
    gauss = jnp.where(inside, jnp.exp(minus * freq), 0.0) * (1.0 / math.sqrt(P_SIZE * NF))
    ratio = jnp.exp(minus * ((LANES // P_SIZE) * omega_step / width_scale))
    for group in range(GROUPS):
        lanes = slice(group * LANES, (group + 1) * LANES)
        yield jnp.concatenate(
            [(gauss * beam_re[:, lanes]).astype(bf16), (gauss * beam_im[:, lanes]).astype(bf16)],
            axis=1,
        )
        gauss = gauss * ratio


def contributions(windows, u_ref):
    blocks = []
    for _ in u_groups(u_ref.at[0], *windows[0][:2]):
        pass
    for i, window in enumerate(windows):
        following = iter(())
        if i + 1 < len(windows):
            following = u_groups(u_ref.at[i + 1], *windows[i + 1][:2])
        total = None
        for group, v in enumerate(v_groups(*window[2:])):
            part = dot(v, u_ref[i, pl.ds(group * 2 * LANES, 2 * LANES), :])
            total = part if total is None else total + part
            next(following, None)
        blocks.append(total)
    return blocks


def pack_kernel(place_ref, times_ref, amps_ref, second_ref, third_ref, near_ref):
    place = place_ref[0]

    def pack(w, ref):
        ref[0:P_SIZE] = times_ref[w]
        ref[P_SIZE:] = amps_ref[w]

    base = jnp.where(place < GROUP // 2, 0, WIN - place)
    for i in range(HALF):
        pack(jnp.minimum(base + i, WIN - 1), second_ref.at[i])
    pack(jnp.where(place == 1, WIN - 1, 0), third_ref)
    for i in range(GROUP):
        pack(HALF - place + i, near_ref.at[i])


def tails_kernel(place_ref, foot_ref, lateral_ref, tail_ref, flag_ref):
    place = place_ref[0]
    first_chip = place < GROUP // 2
    base = jnp.where(first_chip, HALF + 1 + place, 0)
    windows = [HALF - place + i for i in range(GROUP)]
    windows += [WIN + jnp.minimum(base + i, WIN - 1) for i in range(HALF)]
    windows += [2 * WIN + jnp.where(first_chip, WIN - 1, 0)]
    sub = iota((8, LANES), 0)
    for i, w in enumerate(windows):
        first, end = foot_ref[w, 0].astype(f32), foot_ref[w, 1].astype(f32)
        lateral = jnp.broadcast_to(lateral_ref[pl.ds(w, 1), :], (8, LANES))
        tail_ref[i] = jnp.where(sub == 0, lateral, jnp.where(sub == 1, first, end))
    flag_ref[...] = jnp.full(flag_ref.shape, place.astype(f32))


def unpack(rays, tail):
    return rays[:P_SIZE], rays[P_SIZE:], tail[0:1], tail[1:2], tail[2:3]


def near_kernel(
    arrived_ref, spread_ref, cos_ref, sin_ref, rays_ref, tail_ref, near_ref, beam_ref, u_ref,
    *, scale,
):
    own, second, third = slant_stack(
        arrived_ref[...], spread_ref[...], cos_ref[...], sin_ref[...], scale
    )
    for i, beam in enumerate(second + third):
        beam_ref[i : i + 1] = beam
    windows = [unpack(rays_ref[i], tail_ref[i]) + own for i in range(GROUP)]
    for i, block in enumerate(contributions(windows, u_ref)):
        near_ref[i] = block


def far_kernel(
    flag_ref, tail_ref, near_ref, beam_ref, second_ref, third_0_ref, third_1_ref, out_ref, u_ref,
    *, parts,
):
    second, third = (beam_ref[0:1], beam_ref[1:2]), (beam_ref[2:3], beam_ref[3:4])
    windows = [unpack(second_ref[i], tail_ref[GROUP + i]) + second for i in range(HALF)]
    windows += [unpack(third_0_ref[...] + third_1_ref[...], tail_ref[GROUP + HALF]) + third]
    a, b, c, d = contributions(windows, u_ref)
    rows = out_ref.shape[1]
    place = flag_ref[0:1, :]
    is_0, is_2, is_3 = place == 0.0, place == 2.0, place == 3.0
    first = place < GROUP / 2

    def when(condition, block):
        return jnp.where(condition, block, 0.0)

    totals = (
        near_ref[0] + when(first, a + d),
        near_ref[1] + when(first, b) + when(is_3, a),
        near_ref[2] + when(is_0, c) + when(is_3, b) + when(is_2, a),
        near_ref[3] + when(is_3, c) + when(is_2, b) + when(~first, d),
    )
    for t, total in enumerate(totals):
        total = total.T.astype(bf16)
        for i, o in enumerate(parts):
            out_ref[i * GROUP + t] = total[o * rows : (o + 1) * rows]


def total_kernel(parts_ref, out_ref):
    total = parts_ref[0].astype(f32)
    for i in range(1, parts_ref.shape[0]):
        total = total + parts_ref[i].astype(f32)
    out_ref[...] = total


def vmem():
    return pl.BlockSpec(memory_space=pltpu.VMEM)


def smem():
    return pl.BlockSpec(memory_space=pltpu.SMEM)


def call(kernel, out_shape, in_specs, mib=None, scratch=(), flops=0):
    many = isinstance(out_shape, tuple)
    limit = None if mib is None else mib * 1024 * 1024
    return pl.pallas_call(
        kernel,
        out_shape=out_shape,
        in_specs=in_specs,
        out_specs=tuple(vmem() for _ in out_shape) if many else vmem(),
        scratch_shapes=scratch,
        compiler_params=pltpu.CompilerParams(vmem_limit_bytes=limit),
        cost_estimate=pl.CostEstimate(flops=flops, bytes_accessed=1 << 20, transcendentals=0),
    )


def struct(*shape):
    return jax.ShapeDtypeStruct(shape, bf16)


def struct32(*shape):
    return jax.ShapeDtypeStruct(shape, f32)


def shards(traces, centre_ids, midpoint_bins, ray_times, ray_amps, beam_lateral, footprint):
    slab_axes = ("group", "chip", "core")
    my_slab = lax.axis_index(slab_axes)
    slabs = lax.axis_size(slab_axes)
    offsets = lax.axis_size("offset")
    count = traces.shape[1]
    depth = ray_times.shape[4]
    part = depth // offsets
    high, low = dft_tables()
    groups = [(FIRST_SLAB // GROUP + i) % (slabs // GROUP) for i in range(slabs // GROUP)]
    order = [group * GROUP + i for group in groups for i in range(GROUP)]
    routed = call(functools.partial(route_kernel, groups=groups), struct(slabs * ROWS, LANES), [vmem()] * 5)(
        centre_ids.reshape(1, count), midpoint_bins, traces[0], jnp.asarray(high), jnp.asarray(low)
    )
    arrived = lax.all_to_all(
        routed.reshape(slabs, ROWS, LANES), slab_axes, split_axis=0, concat_axis=0,
        axis_index_groups=[order], tiled=True,
    ).reshape(slabs * ROWS, LANES)

    place = (my_slab % GROUP).astype(jnp.int32).reshape(1)

    def to_those(steps):
        pairs = [(i + steps[i % GROUP], i) for i in range(slabs) if steps[i % GROUP]]
        return [(i, j) for i, j in pairs if 0 <= i < slabs]

    ray_rows = 2 * P_SIZE
    u_rows = 2 * P_SIZE * NF
    second_rays, third_rays, near_rays = call(
        pack_kernel,
        (
            struct32(HALF, ray_rows, depth), struct32(ray_rows, depth),
            struct32(GROUP, ray_rows, depth),
        ),
        [smem()] + [vmem()] * 2,
        8,
        flops=1 << 28,
    )(place, ray_times[0, 0], ray_amps[0, 0])
    second_rays = lax.ppermute(second_rays, slab_axes, to_those(SECOND_STEP))
    third_0 = lax.ppermute(third_rays, slab_axes, to_those((THIRD_STEP[0], 0, 0, THIRD_STEP[3])))
    third_1 = lax.ppermute(third_rays, slab_axes, to_those((0, THIRD_STEP[1], THIRD_STEP[2], 0)))

    steps = [jnp.int32(0)] + [
        jnp.asarray(step, jnp.int32)[my_slab % GROUP] for step in (SECOND_STEP, THIRD_STEP)
    ]
    centres = [jnp.clip(my_slab + step, 0, slabs - 1) for step in steps]
    lateral = jnp.concatenate(
        [lax.dynamic_index_in_dim(beam_lateral[0], c, 0, keepdims=False) for c in centres]
    )
    foot = jnp.concatenate(
        [lax.dynamic_index_in_dim(footprint, c, 0, keepdims=False) for c in centres]
    )
    tails, flags = call(
        tails_kernel,
        (struct32(GROUP + HALF + 1, 8, LANES), struct32(8, depth)),
        [smem()] * 2 + [vmem()],
        8,
        flops=1 << 28,
    )(place, foot, jnp.tile(lateral, (1, LANES // P_SIZE)))

    cosine, sine, spread = slant_tables()
    near, beams = call(
        functools.partial(near_kernel, scale=1.0 / math.sqrt(NT * count)),
        (struct32(GROUP, XW, depth), struct32(4, NF * P_SIZE)),
        [vmem()] * 6,
        24,
        [pltpu.VMEM((GROUP, u_rows, depth), bf16)],
    )(
        arrived, jnp.asarray(spread), jnp.asarray(cosine), jnp.asarray(sine), near_rays, tails
    )
    parts = [(FIRST_OFFSET + i) % offsets for i in range(offsets)]
    merged = call(
        functools.partial(far_kernel, parts=parts),
        struct(GROUP * offsets, part, XW),
        [vmem()] * 7,
        24,
        [pltpu.VMEM((HALF + 1, u_rows, depth), bf16)],
    )(flags, tails, near, beams, second_rays, third_0, third_1)
    parts = lax.all_to_all(
        merged, ("offset", "chip", "core"), split_axis=0, concat_axis=0,
        axis_index_groups=[[o * GROUP + t for o in parts for t in range(GROUP)]], tiled=True,
    )
    return call(total_kernel, struct32(part, XW), [vmem()], 4)(parts)


def solution(mesh):
    offsets, slabs = mesh.devices.shape
    shape = (offsets, slabs // GROUP, GROUP // 2, 2)
    chips = Mesh(mesh.devices.reshape(shape), ("offset", "group", "chip", "core"))
    slab = ("group", "chip", "core")
    return jax.shard_map(
        shards,
        mesh=chips,
        in_specs=(
            P("offset", slab, None),
            P("offset", slab, None),
            P("offset", slab),
            P("offset", slab, None, None, None),
            P("offset", slab, None, None, None),
            P("offset", None, None, None),
            P(),
        ),
        out_specs=P("offset", slab),
        check_vma=False,
    )
```

```python
import functools
import math

import jax
import jax.numpy as jnp
import numpy as np
from jax import lax
from jax.experimental import pallas as pl
from jax.experimental.pallas import tpu as pltpu
from jax.sharding import Mesh
from jax.sharding import PartitionSpec as P

NT = 256
NF = 64
KLO = 8
P_SIZE = 16
BINS = 16
CAP = 6
WIN = 7
XW = 128
ROWS = 16
LANES = 128
HALF = (WIN - 1) // 2
GROUPS = P_SIZE * NF // LANES
GROUP = 4
FIRST_SLAB = 52
READY = 2
FIRST_OFFSET = 6
SECOND_STEP = (-1, -3, 3, 1)
THIRD_STEP = (-3, -4, 4, 3)
THIRD_SLOT = (0, 3, 3, 0)

two_pi = 2.0 * math.pi
slow_step = 0.25
width_scale = 200.0
omega_step = two_pi / NT

f32 = jnp.float32
bf16 = jnp.bfloat16


def dft_tables():
    sample = np.arange(NT)[:, None]
    turns = (sample * (np.arange(NF)[None, :] + KLO) % NT) * (two_pi / NT)
    table = np.concatenate([np.cos(turns), -np.sin(turns)], axis=1).astype(np.float32)
    high = table.astype(bf16)
    low = (table - high.astype(np.float32)).astype(bf16)
    return high, low


def slant_tables():
    freq = (np.arange(NF) + KLO) * omega_step
    slow = (np.arange(P_SIZE) - (P_SIZE - 1) / 2.0) * slow_step
    place = np.arange(BINS) - (BINS - 1) / 2.0
    phase = place[:, None, None] * freq[None, :, None] * slow[None, None, :]
    phase = phase.reshape(BINS, NF * P_SIZE)
    spread = np.arange(2 * NF)[:, None] % NF == np.arange(NF * P_SIZE)[None, :] // P_SIZE
    return (
        np.cos(phase).astype(np.float32),
        np.sin(phase).astype(np.float32),
        spread.astype(np.float32).astype(bf16),
    )


def iota(shape, dim):
    return lax.broadcasted_iota(jnp.int32, shape, dim)


def dot(a, b):
    return jnp.dot(a, b, preferred_element_type=f32)


def by_place(place, choices):
    value = choices[-1]
    for i in reversed(range(len(choices) - 1)):
        value = jnp.where(place == i, choices[i], value)
    return value


def route_kernel(ids_ref, bins_ref, traces_ref, high_ref, low_ref, out_ref, *, groups):
    count = traces_ref.shape[0]
    square = (count, count)
    row, col = iota(square, 0), iota(square, 1)
    ids_across = ids_ref[...]
    ids_down = jnp.sum(
        jnp.where(row == col, ids_across.astype(f32), 0.0), axis=1, keepdims=True
    )
    same = ids_down == ids_across.astype(f32)
    rank_across = jnp.sum(jnp.where(same & (row < col), 1.0, 0.0), axis=0, keepdims=True)
    code_across = ids_across * 8 + rank_across.astype(jnp.int32)
    place_across = bins_ref[...].astype(f32) - (BINS - 1) / 2.0
    place_down = jnp.sum(jnp.where(row == col, place_across, 0.0), axis=1, keepdims=True)
    traces = traces_ref[...]
    spectrum = dot(traces, high_ref[...]) + dot(traces, low_ref[...])
    values = jnp.concatenate([spectrum, jnp.broadcast_to(place_down, square)], axis=1).astype(bf16)

    group_rows = GROUP * ROWS
    slot = iota((group_rows, count), 0) % ROWS
    slab = iota((group_rows, count), 0) // ROWS
    second = (slab + by_place(slab, SECOND_STEP)) * 8 + slot - CAP
    third = (slab + by_place(slab, THIRD_STEP)) * 8 + slot - 2 * CAP
    third = third + by_place(slab, THIRD_SLOT)
    wanted = jnp.where(slot < CAP, slab * 8 + slot, jnp.where(slot < 2 * CAP, second, third))
    wanted = jnp.where(slot == ROWS - 1, -(1 << 20), wanted)
    pick = [
        jnp.where(wanted + group * GROUP * 8 == code_across, 1.0, 0.0).astype(bf16)
        for group in groups
    ]
    picked = dot(jnp.concatenate(pick, axis=0), values).reshape(-1, ROWS, 2 * LANES)
    shape = picked.shape[:2] + (LANES,)
    places = jnp.where(iota(shape, 1) == iota(shape, 2), picked[:, :, LANES:], 0.0)
    places = jnp.broadcast_to(jnp.sum(places, axis=1, keepdims=True), shape)
    block = jnp.where(iota(shape, 1) == ROWS - 1, places, picked[:, :, :LANES])
    out_ref[...] = block.reshape(out_ref.shape).astype(bf16)


def slant_stack(arrived, spread, cosine, sine, scale):
    rows = arrived.shape[0]
    shape = (rows // ROWS, ROWS, LANES)
    full = arrived.astype(f32).reshape(shape)
    last = jnp.broadcast_to(full[:, ROWS - 1 :, :], shape)
    own = jnp.where(iota(shape, 1) == iota(shape, 2), last, 0.0).reshape(rows, LANES).astype(bf16)
    place = dot(own, jnp.ones((LANES, LANES), bf16))
    lane, slot = iota((rows, LANES), 1), iota((rows, LANES), 0) % ROWS
    centre = jnp.where(slot < CAP, 0, jnp.where(slot < 2 * CAP, 1, 2))
    bin_place = (lane % BINS).astype(f32) - (BINS - 1) / 2.0
    hit = (place == bin_place) & (lane // BINS == centre) & (slot < ROWS - 1)
    in_bin = jnp.where(hit, 1.0, 0.0).astype(bf16)
    number = 3 * BINS
    binned = lax.dot_general(
        in_bin, arrived, (((0,), (0,)), ((), ())), preferred_element_type=f32
    )[:number]
    real = iota((number, LANES), 1) < NF
    parts = []
    for part in (jnp.where(real, binned, 0.0), jnp.where(real, 0.0, binned)):
        high = part.astype(bf16)
        parts += [high, (part - high.astype(f32)).astype(bf16)]
    wide = dot(jnp.concatenate(parts, axis=0), spread)
    wide_re = wide[:number] + wide[number : 2 * number]
    wide_im = wide[2 * number : 3 * number] + wide[3 * number :]
    beams = []
    for first in range(0, number, BINS):
        re, im = wide_re[first : first + BINS], wide_im[first : first + BINS]
        beam_re = jnp.sum(re * cosine + im * sine, axis=0, keepdims=True)
        beam_im = jnp.sum(im * cosine - re * sine, axis=0, keepdims=True)
        beams.append(
            (
                (beam_re * scale).astype(bf16).astype(f32),
                (beam_im * scale).astype(bf16).astype(f32),
            )
        )
    return beams


def cos_sin_turns(turns):
    half = (turns - 0.5) * math.pi
    sq = half * half
    sin_of = 1.0 / 6227020800.0
    for divisor in (-39916800.0, 362880.0, -5040.0, 120.0, -6.0, 1.0):
        sin_of = sin_of * sq + 1.0 / divisor
    sin_of = sin_of * half
    cos_of = 1.0 / 479001600.0
    for divisor in (-3628800.0, 40320.0, -720.0, 24.0, -2.0, 1.0):
        cos_of = cos_of * sq + 1.0 / divisor
    return 2.0 * sin_of * sin_of - 1.0, -2.0 * sin_of * cos_of


def u_groups(u_ref, times, amps):
    def times_of(a, b):
        return a[0] * b[0] - a[1] * b[1], a[0] * b[1] + a[1] * b[0]

    one = cos_sin_turns(times * (1.0 / NT))
    two = times_of(one, one)
    four = times_of(two, two)
    eight = times_of(four, four)
    start = (amps * eight[0], amps * eight[1])
    walk = [start, times_of(start, one), times_of(start, two)]
    walk.append(times_of(walk[1], two))
    values = [(c, -s) for c, s in walk]
    factor = 2.0 * two[0]
    for j in range(NF):
        if j >= 4:
            values.append(
                tuple(factor * values[j - 2][i] - values[j - 4][i] for i in range(2))
            )
        group, inner = divmod(j, LANES // P_SIZE)
        for i in range(2):
            first = group * 2 * LANES + i * LANES + inner * P_SIZE
            u_ref[pl.ds(first, P_SIZE), :] = values[j][i].astype(bf16)
        if inner == LANES // P_SIZE - 1:
            yield


def v_groups(lateral, first, end, beam_re, beam_im):
    xs = iota((XW, LANES), 0).astype(f32)
    freq = (iota((XW, LANES), 1) // P_SIZE + KLO).astype(f32) * (omega_step / width_scale)
    away = xs - lateral
    minus = -(away * away)
    inside = (xs >= first) & (xs < end)
    gauss = jnp.where(inside, jnp.exp(minus * freq), 0.0) * (1.0 / math.sqrt(P_SIZE * NF))
    ratio = jnp.exp(minus * ((LANES // P_SIZE) * omega_step / width_scale))
    for group in range(GROUPS):
        lanes = slice(group * LANES, (group + 1) * LANES)
        yield jnp.concatenate(
            [(gauss * beam_re[:, lanes]).astype(bf16), (gauss * beam_im[:, lanes]).astype(bf16)],
            axis=1,
        )
        gauss = gauss * ratio


def contributions(windows, u_ref, ready_ref=None):
    blocks = []
    ready = 0 if ready_ref is None else ready_ref.shape[0]
    later = [
        u_groups(u_ref.at[i - ready], *windows[i][:2]) for i in range(ready, len(windows))
    ]
    if not ready:
        for _ in later.pop(0):
            pass
    for i, window in enumerate(windows):
        following = later.pop(0) if later else iter(())
        held = ready_ref.at[i] if i < ready else u_ref.at[i - ready]
        total = None
        for group, v in enumerate(v_groups(*window[2:])):
            part = dot(v, held[pl.ds(group * 2 * LANES, 2 * LANES), :])
            total = part if total is None else total + part
            next(following, None)
        blocks.append(total)
    return blocks


def u_kernel(rays_ref, out_ref):
    for i in range(out_ref.shape[0]):
        for _ in u_groups(out_ref.at[i], rays_ref[i, :P_SIZE], rays_ref[i, P_SIZE:]):
            pass


def pack_kernel(place_ref, times_ref, amps_ref, second_ref, third_ref, near_ref):
    place = place_ref[0]

    def pack(w, ref):
        ref[0:P_SIZE] = times_ref[w]
        ref[P_SIZE:] = amps_ref[w]

    base = jnp.where(place < GROUP // 2, 0, WIN - place)
    for i in range(HALF):
        pack(jnp.minimum(base + i, WIN - 1), second_ref.at[i])
    pack(jnp.where(place == 1, WIN - 1, 0), third_ref)
    for i in range(GROUP):
        pack(HALF - place + i, near_ref.at[i])


def tails_kernel(slab_ref, foot_ref, lateral_ref, tail_ref, flag_ref):
    slab = slab_ref[0]
    place = slab % GROUP
    first_chip = place < GROUP // 2
    base = jnp.where(first_chip, HALF + 1 + place, 0)
    second = slab + by_place(place, SECOND_STEP)
    third = slab + by_place(place, THIRD_STEP)
    windows = [(slab, HALF - place + i) for i in range(GROUP)]
    windows += [(second, jnp.minimum(base + i, WIN - 1)) for i in range(HALF)]
    windows += [(third, jnp.where(first_chip, WIN - 1, 0))]
    slabs = lateral_ref.shape[2]
    spread = iota((P_SIZE, LANES), 1) % P_SIZE == iota((P_SIZE, LANES), 0)
    sub = iota((8, LANES), 0)
    for i, (centre, w) in enumerate(windows):
        lateral = jnp.where(iota((P_SIZE, slabs), 1) == centre, lateral_ref[w], 0.0)
        lateral = jnp.sum(lateral, axis=1, keepdims=True)
        lateral = jnp.sum(jnp.where(spread, lateral, 0.0), axis=0, keepdims=True)
        foot = jnp.where(iota((2, slabs), 1) == centre, foot_ref[w].astype(f32), 0.0)
        foot = jnp.sum(foot, axis=1, keepdims=True)
        tail_ref[i] = jnp.where(sub == 0, lateral, jnp.where(sub == 1, foot[0:1], foot[1:2]))
    flag_ref[...] = jnp.full(flag_ref.shape, place.astype(f32))


def unpack(rays, tail):
    return rays[:P_SIZE], rays[P_SIZE:], tail[0:1], tail[1:2], tail[2:3]


def near_kernel(
    arrived_ref, spread_ref, cos_ref, sin_ref, rays_ref, tail_ref, ready_ref, near_ref, beam_ref, u_ref,
    *, scale,
):
    own, second, third = slant_stack(
        arrived_ref[...], spread_ref[...], cos_ref[...], sin_ref[...], scale
    )
    for i, beam in enumerate(second + third):
        beam_ref[i : i + 1] = beam
    windows = [unpack(rays_ref[i], tail_ref[i]) + own for i in range(GROUP)]
    for i, block in enumerate(contributions(windows, u_ref, ready_ref)):
        near_ref[i] = block


def far_kernel(
    flag_ref, tail_ref, near_ref, beam_ref, second_ref, third_0_ref, third_1_ref, out_ref, u_ref,
    *, parts,
):
    second, third = (beam_ref[0:1], beam_ref[1:2]), (beam_ref[2:3], beam_ref[3:4])
    windows = [unpack(second_ref[i], tail_ref[GROUP + i]) + second for i in range(HALF)]
    windows += [unpack(third_0_ref[...] + third_1_ref[...], tail_ref[GROUP + HALF]) + third]
    a, b, c, d = contributions(windows, u_ref)
    rows = out_ref.shape[1]
    place = flag_ref[0:1, :]
    is_0, is_2, is_3 = place == 0.0, place == 2.0, place == 3.0
    first = place < GROUP / 2

    def when(condition, block):
        return jnp.where(condition, block, 0.0)

    totals = (
        near_ref[0] + when(first, a + d),
        near_ref[1] + when(first, b) + when(is_3, a),
        near_ref[2] + when(is_0, c) + when(is_3, b) + when(is_2, a),
        near_ref[3] + when(is_3, c) + when(is_2, b) + when(~first, d),
    )
    for t, total in enumerate(totals):
        total = total.T.astype(bf16)
        for i, o in enumerate(parts):
            out_ref[i * GROUP + t] = total[o * rows : (o + 1) * rows]


def total_kernel(parts_ref, out_ref):
    total = parts_ref[0].astype(f32)
    for i in range(1, parts_ref.shape[0]):
        total = total + parts_ref[i].astype(f32)
    out_ref[...] = total


def vmem():
    return pl.BlockSpec(memory_space=pltpu.VMEM)


def smem():
    return pl.BlockSpec(memory_space=pltpu.SMEM)


def call(kernel, out_shape, in_specs, mib=None, scratch=(), flops=0):
    many = isinstance(out_shape, tuple)
    limit = None if mib is None else mib * 1024 * 1024
    return pl.pallas_call(
        kernel,
        out_shape=out_shape,
        in_specs=in_specs,
        out_specs=tuple(vmem() for _ in out_shape) if many else vmem(),
        scratch_shapes=scratch,
        compiler_params=pltpu.CompilerParams(vmem_limit_bytes=limit),
        cost_estimate=pl.CostEstimate(flops=flops, bytes_accessed=1 << 20, transcendentals=0),
    )


def struct(*shape):
    return jax.ShapeDtypeStruct(shape, bf16)


def struct32(*shape):
    return jax.ShapeDtypeStruct(shape, f32)


def shards(traces, centre_ids, midpoint_bins, ray_times, ray_amps, beam_lateral, footprint):
    slab_axes = ("group", "chip", "core")
    my_slab = lax.axis_index(slab_axes)
    slabs = lax.axis_size(slab_axes)
    offsets = lax.axis_size("offset")
    count = traces.shape[1]
    depth = ray_times.shape[4]
    part = depth // offsets
    high, low = dft_tables()
    groups = [(FIRST_SLAB // GROUP + i) % (slabs // GROUP) for i in range(slabs // GROUP)]
    order = [group * GROUP + i for group in groups for i in range(GROUP)]
    routed = call(functools.partial(route_kernel, groups=groups), struct(slabs * ROWS, LANES), [vmem()] * 5)(
        centre_ids.reshape(1, count), midpoint_bins, traces[0], jnp.asarray(high), jnp.asarray(low)
    )
    arrived = lax.all_to_all(
        routed.reshape(slabs, ROWS, LANES), slab_axes, split_axis=0, concat_axis=0,
        axis_index_groups=[order], tiled=True,
    ).reshape(slabs * ROWS, LANES)

    place = (my_slab % GROUP).astype(jnp.int32).reshape(1)

    def to_those(steps):
        pairs = [(i + steps[i % GROUP], i) for i in range(slabs) if steps[i % GROUP]]
        return [(i, j) for i, j in pairs if 0 <= i < slabs]

    ray_rows = 2 * P_SIZE
    u_rows = 2 * P_SIZE * NF
    second_rays, third_rays, near_rays = call(
        pack_kernel,
        (
            struct32(HALF, ray_rows, depth), struct32(ray_rows, depth),
            struct32(GROUP, ray_rows, depth),
        ),
        [smem()] + [vmem()] * 2,
        8,
        flops=1 << 28,
    )(place, ray_times[0, 0], ray_amps[0, 0])
    second_rays = lax.ppermute(second_rays, slab_axes, to_those(SECOND_STEP))
    third_0 = lax.ppermute(third_rays, slab_axes, to_those((THIRD_STEP[0], 0, 0, THIRD_STEP[3])))
    third_1 = lax.ppermute(third_rays, slab_axes, to_those((0, THIRD_STEP[1], THIRD_STEP[2], 0)))

    tails, flags = call(
        tails_kernel,
        (struct32(GROUP + HALF + 1, 8, LANES), struct32(8, depth)),
        [smem()] + [vmem()] * 2,
        8,
        flops=1 << 28,
    )(
        my_slab.astype(jnp.int32).reshape(1),
        footprint.transpose(1, 2, 0),
        beam_lateral[0].transpose(1, 2, 0),
    )

    cosine, sine, spread = slant_tables()
    ready = call(u_kernel, struct(READY, u_rows, depth), [vmem()], 8, flops=1 << 28)(near_rays)
    near, beams = call(
        functools.partial(near_kernel, scale=1.0 / math.sqrt(NT * count)),
        (struct32(GROUP, XW, depth), struct32(4, NF * P_SIZE)),
        [vmem()] * 7,
        24,
        [pltpu.VMEM((GROUP - READY, u_rows, depth), bf16)],
    )(
        arrived, jnp.asarray(spread), jnp.asarray(cosine), jnp.asarray(sine), near_rays, tails,
        ready,
    )
    parts = [(FIRST_OFFSET + i) % offsets for i in range(offsets)]
    merged = call(
        functools.partial(far_kernel, parts=parts),
        struct(GROUP * offsets, part, XW),
        [vmem()] * 7,
        24,
        [pltpu.VMEM((HALF + 1, u_rows, depth), bf16)],
    )(flags, tails, near, beams, second_rays, third_0, third_1)
    parts = lax.all_to_all(
        merged, ("offset", "chip", "core"), split_axis=0, concat_axis=0,
        axis_index_groups=[[o * GROUP + t for o in parts for t in range(GROUP)]], tiled=True,
    )
    return call(total_kernel, struct32(part, XW), [vmem()], 4)(parts)


def solution(mesh):
    offsets, slabs = mesh.devices.shape
    shape = (offsets, slabs // GROUP, GROUP // 2, 2)
    chips = Mesh(mesh.devices.reshape(shape), ("offset", "group", "chip", "core"))
    slab = ("group", "chip", "core")
    return jax.shard_map(
        shards,
        mesh=chips,
        in_specs=(
            P("offset", slab, None),
            P("offset", slab, None),
            P("offset", slab),
            P("offset", slab, None, None, None),
            P("offset", slab, None, None, None),
            P("offset", None, None, None),
            P(),
        ),
        out_specs=P("offset", slab),
        check_vma=False,
    )
```

```python
import functools
import math

import jax
import jax.numpy as jnp
import numpy as np
from jax import lax
from jax.experimental import pallas as pl
from jax.experimental.pallas import tpu as pltpu
from jax.sharding import Mesh
from jax.sharding import PartitionSpec as P

NT = 256
NF = 64
KLO = 8
P_SIZE = 16
BINS = 16
CAP = 6
WIN = 7
XW = 128
ROWS = 16
LANES = 128
HALF = (WIN - 1) // 2
GROUPS = P_SIZE * NF // LANES
GROUP = 4
FIRST_SLAB = 54
READY = 2
FIRST_OFFSET = 6
SECOND_STEP = (-1, -3, 3, 1)
THIRD_STEP = (-3, -4, 4, 3)
THIRD_SLOT = (0, 3, 3, 0)

two_pi = 2.0 * math.pi
slow_step = 0.25
width_scale = 200.0
omega_step = two_pi / NT

f32 = jnp.float32
bf16 = jnp.bfloat16


def dft_tables():
    sample = np.arange(NT)[:, None]
    turns = (sample * (np.arange(NF)[None, :] + KLO) % NT) * (two_pi / NT)
    table = np.concatenate([np.cos(turns), -np.sin(turns)], axis=1).astype(np.float32)
    high = table.astype(bf16)
    low = (table - high.astype(np.float32)).astype(bf16)
    return high, low


def slant_tables():
    freq = (np.arange(NF) + KLO) * omega_step
    slow = (np.arange(P_SIZE) - (P_SIZE - 1) / 2.0) * slow_step
    place = np.arange(BINS) - (BINS - 1) / 2.0
    phase = place[:, None, None] * freq[None, :, None] * slow[None, None, :]
    phase = phase.reshape(BINS, NF * P_SIZE)
    spread = np.arange(2 * NF)[:, None] % NF == np.arange(NF * P_SIZE)[None, :] // P_SIZE
    return (
        np.cos(phase).astype(np.float32),
        np.sin(phase).astype(np.float32),
        spread.astype(np.float32).astype(bf16),
    )


def iota(shape, dim):
    return lax.broadcasted_iota(jnp.int32, shape, dim)


def dot(a, b):
    return jnp.dot(a, b, preferred_element_type=f32)


def by_place(place, choices):
    value = choices[-1]
    for i in reversed(range(len(choices) - 1)):
        value = jnp.where(place == i, choices[i], value)
    return value


def route_kernel(ids_ref, bins_ref, traces_ref, high_ref, low_ref, out_ref, *, groups):
    count = traces_ref.shape[0]
    square = (count, count)
    row, col = iota(square, 0), iota(square, 1)
    ids_across = ids_ref[...]
    ids_down = jnp.sum(
        jnp.where(row == col, ids_across.astype(f32), 0.0), axis=1, keepdims=True
    )
    same = ids_down == ids_across.astype(f32)
    rank_across = jnp.sum(jnp.where(same & (row < col), 1.0, 0.0), axis=0, keepdims=True)
    code_across = ids_across * 8 + rank_across.astype(jnp.int32)
    place_across = bins_ref[...].astype(f32) - (BINS - 1) / 2.0
    place_down = jnp.sum(jnp.where(row == col, place_across, 0.0), axis=1, keepdims=True)
    traces = traces_ref[...]
    spectrum = dot(traces, high_ref[...]) + dot(traces, low_ref[...])
    values = jnp.concatenate([spectrum, jnp.broadcast_to(place_down, square)], axis=1).astype(bf16)

    group_rows = GROUP * ROWS
    slot = iota((group_rows, count), 0) % ROWS
    slab = iota((group_rows, count), 0) // ROWS
    second = (slab + by_place(slab, SECOND_STEP)) * 8 + slot - CAP
    third = (slab + by_place(slab, THIRD_STEP)) * 8 + slot - 2 * CAP
    third = third + by_place(slab, THIRD_SLOT)
    wanted = jnp.where(slot < CAP, slab * 8 + slot, jnp.where(slot < 2 * CAP, second, third))
    wanted = jnp.where(slot == ROWS - 1, -(1 << 20), wanted)
    pick = [
        jnp.where(wanted + group * GROUP * 8 == code_across, 1.0, 0.0).astype(bf16)
        for group in groups
    ]
    pick = jnp.concatenate(pick, axis=0)
    skip = FIRST_SLAB % GROUP * ROWS
    if skip:
        pick = jnp.concatenate([pick[skip:], pick[:skip]], axis=0)
    picked = dot(pick, values).reshape(-1, ROWS, 2 * LANES)
    shape = picked.shape[:2] + (LANES,)
    places = jnp.where(iota(shape, 1) == iota(shape, 2), picked[:, :, LANES:], 0.0)
    places = jnp.broadcast_to(jnp.sum(places, axis=1, keepdims=True), shape)
    block = jnp.where(iota(shape, 1) == ROWS - 1, places, picked[:, :, :LANES])
    out_ref[...] = block.reshape(out_ref.shape).astype(bf16)


def slant_stack(arrived, spread, cosine, sine, scale):
    rows = arrived.shape[0]
    shape = (rows // ROWS, ROWS, LANES)
    full = arrived.astype(f32).reshape(shape)
    last = jnp.broadcast_to(full[:, ROWS - 1 :, :], shape)
    own = jnp.where(iota(shape, 1) == iota(shape, 2), last, 0.0).reshape(rows, LANES).astype(bf16)
    place = dot(own, jnp.ones((LANES, LANES), bf16))
    lane, slot = iota((rows, LANES), 1), iota((rows, LANES), 0) % ROWS
    centre = jnp.where(slot < CAP, 0, jnp.where(slot < 2 * CAP, 1, 2))
    bin_place = (lane % BINS).astype(f32) - (BINS - 1) / 2.0
    hit = (place == bin_place) & (lane // BINS == centre) & (slot < ROWS - 1)
    in_bin = jnp.where(hit, 1.0, 0.0).astype(bf16)
    number = 3 * BINS
    binned = lax.dot_general(
        in_bin, arrived, (((0,), (0,)), ((), ())), preferred_element_type=f32
    )[:number]
    real = iota((number, LANES), 1) < NF
    parts = []
    for part in (jnp.where(real, binned, 0.0), jnp.where(real, 0.0, binned)):
        high = part.astype(bf16)
        parts += [high, (part - high.astype(f32)).astype(bf16)]
    wide = dot(jnp.concatenate(parts, axis=0), spread)
    wide_re = wide[:number] + wide[number : 2 * number]
    wide_im = wide[2 * number : 3 * number] + wide[3 * number :]
    beams = []
    for first in range(0, number, BINS):
        re, im = wide_re[first : first + BINS], wide_im[first : first + BINS]
        beam_re = jnp.sum(re * cosine + im * sine, axis=0, keepdims=True)
        beam_im = jnp.sum(im * cosine - re * sine, axis=0, keepdims=True)
        beams.append(
            (
                (beam_re * scale).astype(bf16).astype(f32),
                (beam_im * scale).astype(bf16).astype(f32),
            )
        )
    return beams


def cos_sin_turns(turns):
    half = (turns - 0.5) * math.pi
    sq = half * half
    sin_of = 1.0 / 6227020800.0
    for divisor in (-39916800.0, 362880.0, -5040.0, 120.0, -6.0, 1.0):
        sin_of = sin_of * sq + 1.0 / divisor
    sin_of = sin_of * half
    cos_of = 1.0 / 479001600.0
    for divisor in (-3628800.0, 40320.0, -720.0, 24.0, -2.0, 1.0):
        cos_of = cos_of * sq + 1.0 / divisor
    return 2.0 * sin_of * sin_of - 1.0, -2.0 * sin_of * cos_of


def u_groups(u_ref, times, amps):
    def times_of(a, b):
        return a[0] * b[0] - a[1] * b[1], a[0] * b[1] + a[1] * b[0]

    cos_1, sin_1 = cos_sin_turns(times * (1.0 / NT))
    one = (cos_1, -sin_1)
    two = times_of(one, one)
    four = times_of(two, two)
    eight = times_of(four, four)
    first = (amps * eight[0], amps * eight[1])
    second = times_of(first, one)
    factor = 2.0 * cos_1
    number = LANES // P_SIZE
    for group in range(GROUPS):
        if group:
            first, second = times_of(first, eight), times_of(second, eight)
        values = [first, second]
        for inner in range(number):
            if inner >= 2:
                values.append(
                    tuple(factor * values[-1][i] - values[-2][i] for i in range(2))
                )
            for i in range(2):
                row = group * 2 * LANES + i * LANES + inner * P_SIZE
                u_ref[pl.ds(row, P_SIZE), :] = values[inner][i].astype(bf16)
        yield


def v_groups(lateral, first, end, beam_re, beam_im):
    xs = iota((XW, LANES), 0).astype(f32)
    freq = (iota((XW, LANES), 1) // P_SIZE + KLO).astype(f32) * (omega_step / width_scale)
    away = xs - lateral
    minus = -(away * away)
    inside = (xs >= first) & (xs < end)
    gauss = jnp.where(inside, jnp.exp(minus * freq), 0.0) * (1.0 / math.sqrt(P_SIZE * NF))
    ratio = jnp.exp(minus * ((LANES // P_SIZE) * omega_step / width_scale))
    for group in range(GROUPS):
        lanes = slice(group * LANES, (group + 1) * LANES)
        yield jnp.concatenate(
            [(gauss * beam_re[:, lanes]).astype(bf16), (gauss * beam_im[:, lanes]).astype(bf16)],
            axis=1,
        )
        gauss = gauss * ratio


def contributions(windows, u_ref, ready_ref=None):
    blocks = []
    ready = 0 if ready_ref is None else ready_ref.shape[0]
    later = [
        u_groups(u_ref.at[i - ready], *windows[i][:2]) for i in range(ready, len(windows))
    ]
    if not ready:
        for _ in later.pop(0):
            pass
    for i, window in enumerate(windows):
        following = later.pop(0) if later else iter(())
        held = ready_ref.at[i] if i < ready else u_ref.at[i - ready]
        total = None
        for group, v in enumerate(v_groups(*window[2:])):
            part = dot(v, held[pl.ds(group * 2 * LANES, 2 * LANES), :])
            total = part if total is None else total + part
            next(following, None)
        blocks.append(total)
    return blocks


def u_kernel(rays_ref, out_ref):
    for i in range(out_ref.shape[0]):
        for _ in u_groups(out_ref.at[i], rays_ref[i, :P_SIZE], rays_ref[i, P_SIZE:]):
            pass


def pack_kernel(place_ref, times_ref, amps_ref, second_ref, third_ref, near_ref):
    place = place_ref[0]

    def pack(w, ref):
        ref[0:P_SIZE] = times_ref[w]
        ref[P_SIZE:] = amps_ref[w]

    base = jnp.where(place < GROUP // 2, 0, WIN - place)
    for i in range(HALF):
        pack(jnp.minimum(base + i, WIN - 1), second_ref.at[i])
    pack(jnp.where(place == 1, WIN - 1, 0), third_ref)
    for i in range(GROUP):
        pack(HALF - place + i, near_ref.at[i])


def tails_kernel(slab_ref, foot_ref, lateral_ref, tail_ref, flag_ref):
    slab = slab_ref[0]
    place = slab % GROUP
    first_chip = place < GROUP // 2
    base = jnp.where(first_chip, HALF + 1 + place, 0)
    second = slab + by_place(place, SECOND_STEP)
    third = slab + by_place(place, THIRD_STEP)
    windows = [(slab, HALF - place + i) for i in range(GROUP)]
    windows += [(second, jnp.minimum(base + i, WIN - 1)) for i in range(HALF)]
    windows += [(third, jnp.where(first_chip, WIN - 1, 0))]
    slabs = lateral_ref.shape[2]
    spread = iota((P_SIZE, LANES), 1) % P_SIZE == iota((P_SIZE, LANES), 0)
    sub = iota((8, LANES), 0)
    for i, (centre, w) in enumerate(windows):
        lateral = jnp.where(iota((P_SIZE, slabs), 1) == centre, lateral_ref[w], 0.0)
        lateral = jnp.sum(lateral, axis=1, keepdims=True)
        lateral = jnp.sum(jnp.where(spread, lateral, 0.0), axis=0, keepdims=True)
        foot = jnp.where(iota((2, slabs), 1) == centre, foot_ref[w].astype(f32), 0.0)
        foot = jnp.sum(foot, axis=1, keepdims=True)
        tail_ref[i] = jnp.where(sub == 0, lateral, jnp.where(sub == 1, foot[0:1], foot[1:2]))
    flag_ref[...] = jnp.full(flag_ref.shape, place.astype(f32))


def unpack(rays, tail):
    return rays[:P_SIZE], rays[P_SIZE:], tail[0:1], tail[1:2], tail[2:3]


def near_kernel(
    arrived_ref, spread_ref, cos_ref, sin_ref, rays_ref, tail_ref, ready_ref, near_ref, beam_ref, u_ref,
    *, scale,
):
    own, second, third = slant_stack(
        arrived_ref[...], spread_ref[...], cos_ref[...], sin_ref[...], scale
    )
    for i, beam in enumerate(second + third):
        beam_ref[i : i + 1] = beam
    windows = [unpack(rays_ref[i], tail_ref[i]) + own for i in range(GROUP)]
    for i, block in enumerate(contributions(windows, u_ref, ready_ref)):
        near_ref[i] = block


def far_kernel(
    flag_ref, tail_ref, near_ref, beam_ref, second_ref, third_0_ref, third_1_ref, out_ref, u_ref,
    *, parts,
):
    second, third = (beam_ref[0:1], beam_ref[1:2]), (beam_ref[2:3], beam_ref[3:4])
    windows = [unpack(second_ref[i], tail_ref[GROUP + i]) + second for i in range(HALF)]
    windows += [unpack(third_0_ref[...] + third_1_ref[...], tail_ref[GROUP + HALF]) + third]
    a, b, c, d = contributions(windows, u_ref)
    rows = out_ref.shape[1]
    place = flag_ref[0:1, :]
    is_0, is_2, is_3 = place == 0.0, place == 2.0, place == 3.0
    first = place < GROUP / 2

    def when(condition, block):
        return jnp.where(condition, block, 0.0)

    totals = (
        near_ref[0] + when(first, a + d),
        near_ref[1] + when(first, b) + when(is_3, a),
        near_ref[2] + when(is_0, c) + when(is_3, b) + when(is_2, a),
        near_ref[3] + when(is_3, c) + when(is_2, b) + when(~first, d),
    )
    for t, total in enumerate(totals):
        total = total.T.astype(bf16)
        for i, o in enumerate(parts):
            out_ref[i * GROUP + t] = total[o * rows : (o + 1) * rows]


def total_kernel(parts_ref, out_ref):
    total = parts_ref[0].astype(f32)
    for i in range(1, parts_ref.shape[0]):
        total = total + parts_ref[i].astype(f32)
    out_ref[...] = total


def vmem():
    return pl.BlockSpec(memory_space=pltpu.VMEM)


def smem():
    return pl.BlockSpec(memory_space=pltpu.SMEM)


def call(kernel, out_shape, in_specs, mib=None, scratch=(), flops=0):
    many = isinstance(out_shape, tuple)
    limit = None if mib is None else mib * 1024 * 1024
    return pl.pallas_call(
        kernel,
        out_shape=out_shape,
        in_specs=in_specs,
        out_specs=tuple(vmem() for _ in out_shape) if many else vmem(),
        scratch_shapes=scratch,
        compiler_params=pltpu.CompilerParams(vmem_limit_bytes=limit),
        cost_estimate=pl.CostEstimate(flops=flops, bytes_accessed=1 << 20, transcendentals=0),
    )


def struct(*shape):
    return jax.ShapeDtypeStruct(shape, bf16)


def struct32(*shape):
    return jax.ShapeDtypeStruct(shape, f32)


def shards(traces, centre_ids, midpoint_bins, ray_times, ray_amps, beam_lateral, footprint):
    slab_axes = ("group", "chip", "core")
    my_slab = lax.axis_index(slab_axes)
    slabs = lax.axis_size(slab_axes)
    offsets = lax.axis_size("offset")
    count = traces.shape[1]
    depth = ray_times.shape[4]
    part = depth // offsets
    high, low = dft_tables()
    groups = [(FIRST_SLAB // GROUP + i) % (slabs // GROUP) for i in range(slabs // GROUP)]
    order = [(FIRST_SLAB + i) % slabs for i in range(slabs)]
    routed = call(functools.partial(route_kernel, groups=groups), struct(slabs * ROWS, LANES), [vmem()] * 5)(
        centre_ids.reshape(1, count), midpoint_bins, traces[0], jnp.asarray(high), jnp.asarray(low)
    )
    arrived = lax.all_to_all(
        routed.reshape(slabs, ROWS, LANES), slab_axes, split_axis=0, concat_axis=0,
        axis_index_groups=[order], tiled=True,
    ).reshape(slabs * ROWS, LANES)

    place = (my_slab % GROUP).astype(jnp.int32).reshape(1)

    def to_those(steps):
        pairs = [(i + steps[i % GROUP], i) for i in range(slabs) if steps[i % GROUP]]
        return [(i, j) for i, j in pairs if 0 <= i < slabs]

    ray_rows = 2 * P_SIZE
    u_rows = 2 * P_SIZE * NF
    second_rays, third_rays, near_rays = call(
        pack_kernel,
        (
            struct32(HALF, ray_rows, depth), struct32(ray_rows, depth),
            struct32(GROUP, ray_rows, depth),
        ),
        [smem()] + [vmem()] * 2,
        8,
        flops=1 << 28,
    )(place, ray_times[0, 0], ray_amps[0, 0])
    second_rays = lax.ppermute(second_rays, slab_axes, to_those(SECOND_STEP))
    third_0 = lax.ppermute(third_rays, slab_axes, to_those((THIRD_STEP[0], 0, 0, THIRD_STEP[3])))
    third_1 = lax.ppermute(third_rays, slab_axes, to_those((0, THIRD_STEP[1], THIRD_STEP[2], 0)))

    tails, flags = call(
        tails_kernel,
        (struct32(GROUP + HALF + 1, 8, LANES), struct32(8, depth)),
        [smem()] + [vmem()] * 2,
        8,
        flops=1 << 28,
    )(
        my_slab.astype(jnp.int32).reshape(1),
        footprint.transpose(1, 2, 0),
        beam_lateral[0].transpose(1, 2, 0),
    )

    cosine, sine, spread = slant_tables()
    ready = call(u_kernel, struct(READY, u_rows, depth), [vmem()], 8, flops=1 << 28)(near_rays)
    near, beams = call(
        functools.partial(near_kernel, scale=1.0 / math.sqrt(NT * count)),
        (struct32(GROUP, XW, depth), struct32(4, NF * P_SIZE)),
        [vmem()] * 7,
        24,
        [pltpu.VMEM((GROUP - READY, u_rows, depth), bf16)],
    )(
        arrived, jnp.asarray(spread), jnp.asarray(cosine), jnp.asarray(sine), near_rays, tails,
        ready,
    )
    parts = [(FIRST_OFFSET + i) % offsets for i in range(offsets)]
    merged = call(
        functools.partial(far_kernel, parts=parts),
        struct(GROUP * offsets, part, XW),
        [vmem()] * 7,
        24,
        [pltpu.VMEM((HALF + 1, u_rows, depth), bf16)],
    )(flags, tails, near, beams, second_rays, third_0, third_1)
    parts = lax.all_to_all(
        merged, ("offset", "chip", "core"), split_axis=0, concat_axis=0,
        axis_index_groups=[[o * GROUP + t for o in parts for t in range(GROUP)]], tiled=True,
    )
    return call(total_kernel, struct32(part, XW), [vmem()], 4)(parts)


def solution(mesh):
    offsets, slabs = mesh.devices.shape
    shape = (offsets, slabs // GROUP, GROUP // 2, 2)
    chips = Mesh(mesh.devices.reshape(shape), ("offset", "group", "chip", "core"))
    slab = ("group", "chip", "core")
    return jax.shard_map(
        shards,
        mesh=chips,
        in_specs=(
            P("offset", slab, None),
            P("offset", slab, None),
            P("offset", slab),
            P("offset", slab, None, None, None),
            P("offset", slab, None, None, None),
            P("offset", None, None, None),
            P(),
        ),
        out_specs=P("offset", slab),
        check_vma=False,
    )
```

```python
import functools
import math

import jax
import jax.numpy as jnp
import numpy as np
from jax import lax
from jax.experimental import pallas as pl
from jax.experimental.pallas import tpu as pltpu
from jax.sharding import Mesh
from jax.sharding import PartitionSpec as P

NT = 256
NF = 64
KLO = 8
P_SIZE = 16
BINS = 16
CAP = 6
WIN = 7
XW = 128
ROWS = 16
LANES = 128
HALF = (WIN - 1) // 2
GROUPS = P_SIZE * NF // LANES
GROUP = 4
FIRST_SLAB = 54
READY = 2
FIRST_OFFSET = 6
SECOND_STEP = (-1, -3, 3, 1)
THIRD_STEP = (-3, -4, 4, 3)
THIRD_SLOT = (0, 3, 3, 0)

two_pi = 2.0 * math.pi
slow_step = 0.25
width_scale = 200.0
omega_step = two_pi / NT

f32 = jnp.float32
bf16 = jnp.bfloat16


def dft_tables():
    sample = np.arange(NT)[:, None]
    turns = (sample * (np.arange(NF)[None, :] + KLO) % NT) * (two_pi / NT)
    table = np.concatenate([np.cos(turns), -np.sin(turns)], axis=1).astype(np.float32)
    high = table.astype(bf16)
    low = (table - high.astype(np.float32)).astype(bf16)
    return high, low


def slant_tables():
    freq = (np.arange(NF) + KLO) * omega_step
    slow = (np.arange(P_SIZE) - (P_SIZE - 1) / 2.0) * slow_step
    place = np.arange(BINS) - (BINS - 1) / 2.0
    phase = place[:, None, None] * freq[None, :, None] * slow[None, None, :]
    phase = phase.reshape(BINS, NF * P_SIZE)
    spread = np.arange(2 * NF)[:, None] % NF == np.arange(NF * P_SIZE)[None, :] // P_SIZE
    return (
        np.cos(phase).astype(np.float32),
        np.sin(phase).astype(np.float32),
        spread.astype(np.float32).astype(bf16),
    )


def iota(shape, dim):
    return lax.broadcasted_iota(jnp.int32, shape, dim)


def dot(a, b):
    return jnp.dot(a, b, preferred_element_type=f32)


def by_place(place, choices):
    value = choices[-1]
    for i in reversed(range(len(choices) - 1)):
        value = jnp.where(place == i, choices[i], value)
    return value


def route_kernel(
    ids_ref, bins_ref, traces_hbm, high_hbm, low_hbm, out_ref, traces_ref, high_ref, low_ref, sems,
    *, groups,
):
    copies = [
        pltpu.make_async_copy(source, target, sems.at[i])
        for i, (source, target) in enumerate(
            ((traces_hbm, traces_ref), (high_hbm, high_ref), (low_hbm, low_ref))
        )
    ]
    for copy in copies:
        copy.start()
    count = traces_ref.shape[0]
    square = (count, count)
    row, col = iota(square, 0), iota(square, 1)
    ids_across = ids_ref[...]
    ids_down = jnp.sum(
        jnp.where(row == col, ids_across.astype(f32), 0.0), axis=1, keepdims=True
    )
    same = ids_down == ids_across.astype(f32)
    rank_across = jnp.sum(jnp.where(same & (row < col), 1.0, 0.0), axis=0, keepdims=True)
    code_across = ids_across * 8 + rank_across.astype(jnp.int32)
    place_across = bins_ref[...].astype(f32) - (BINS - 1) / 2.0
    place_down = jnp.sum(jnp.where(row == col, place_across, 0.0), axis=1, keepdims=True)

    group_rows = GROUP * ROWS
    slot = iota((group_rows, count), 0) % ROWS
    slab = iota((group_rows, count), 0) // ROWS
    second = (slab + by_place(slab, SECOND_STEP)) * 8 + slot - CAP
    third = (slab + by_place(slab, THIRD_STEP)) * 8 + slot - 2 * CAP
    third = third + by_place(slab, THIRD_SLOT)
    wanted = jnp.where(slot < CAP, slab * 8 + slot, jnp.where(slot < 2 * CAP, second, third))
    wanted = jnp.where(slot == ROWS - 1, -(1 << 20), wanted)
    pick = [
        jnp.where(wanted + group * GROUP * 8 == code_across, 1.0, 0.0).astype(bf16)
        for group in groups
    ]
    pick = jnp.concatenate(pick, axis=0)
    skip = FIRST_SLAB % GROUP * ROWS
    if skip:
        pick = jnp.concatenate([pick[skip:], pick[:skip]], axis=0)
    for copy in copies:
        copy.wait()
    traces = traces_ref[...]
    spectrum = dot(traces, high_ref[...]) + dot(traces, low_ref[...])
    values = jnp.concatenate([spectrum, jnp.broadcast_to(place_down, square)], axis=1).astype(bf16)
    picked = dot(pick, values).reshape(-1, ROWS, 2 * LANES)
    shape = picked.shape[:2] + (LANES,)
    places = jnp.where(iota(shape, 1) == iota(shape, 2), picked[:, :, LANES:], 0.0)
    places = jnp.broadcast_to(jnp.sum(places, axis=1, keepdims=True), shape)
    block = jnp.where(iota(shape, 1) == ROWS - 1, places, picked[:, :, :LANES])
    out_ref[...] = block.reshape(out_ref.shape).astype(bf16)


def slant_stack(arrived, spread, cosine, sine, scale):
    rows = arrived.shape[0]
    shape = (rows // ROWS, ROWS, LANES)
    full = arrived.astype(f32).reshape(shape)
    last = jnp.broadcast_to(full[:, ROWS - 1 :, :], shape)
    own = jnp.where(iota(shape, 1) == iota(shape, 2), last, 0.0).reshape(rows, LANES).astype(bf16)
    place = dot(own, jnp.ones((LANES, LANES), bf16))
    lane, slot = iota((rows, LANES), 1), iota((rows, LANES), 0) % ROWS
    centre = jnp.where(slot < CAP, 0, jnp.where(slot < 2 * CAP, 1, 2))
    bin_place = (lane % BINS).astype(f32) - (BINS - 1) / 2.0
    hit = (place == bin_place) & (lane // BINS == centre) & (slot < ROWS - 1)
    in_bin = jnp.where(hit, 1.0, 0.0).astype(bf16)
    number = 3 * BINS
    binned = lax.dot_general(
        in_bin, arrived, (((0,), (0,)), ((), ())), preferred_element_type=f32
    )[:number]
    real = iota((number, LANES), 1) < NF
    parts = []
    for part in (jnp.where(real, binned, 0.0), jnp.where(real, 0.0, binned)):
        high = part.astype(bf16)
        parts += [high, (part - high.astype(f32)).astype(bf16)]
    wide = dot(jnp.concatenate(parts, axis=0), spread)
    wide_re = wide[:number] + wide[number : 2 * number]
    wide_im = wide[2 * number : 3 * number] + wide[3 * number :]
    beams = []
    for first in range(0, number, BINS):
        re, im = wide_re[first : first + BINS], wide_im[first : first + BINS]
        beam_re = jnp.sum(re * cosine + im * sine, axis=0, keepdims=True)
        beam_im = jnp.sum(im * cosine - re * sine, axis=0, keepdims=True)
        beams.append(
            (
                (beam_re * scale).astype(bf16).astype(f32),
                (beam_im * scale).astype(bf16).astype(f32),
            )
        )
    return beams


def cos_sin_turns(turns):
    half = (turns - 0.5) * math.pi
    sq = half * half
    sin_of = 1.0 / 6227020800.0
    for divisor in (-39916800.0, 362880.0, -5040.0, 120.0, -6.0, 1.0):
        sin_of = sin_of * sq + 1.0 / divisor
    sin_of = sin_of * half
    cos_of = 1.0 / 479001600.0
    for divisor in (-3628800.0, 40320.0, -720.0, 24.0, -2.0, 1.0):
        cos_of = cos_of * sq + 1.0 / divisor
    return 2.0 * sin_of * sin_of - 1.0, -2.0 * sin_of * cos_of


def u_groups(u_ref, times, amps):
    def times_of(a, b):
        return a[0] * b[0] - a[1] * b[1], a[0] * b[1] + a[1] * b[0]

    cos_1, sin_1 = cos_sin_turns(times * (1.0 / NT))
    one = (cos_1, -sin_1)
    two = times_of(one, one)
    four = times_of(two, two)
    eight = times_of(four, four)
    first = (amps * eight[0], amps * eight[1])
    second = times_of(first, one)
    factor = 2.0 * cos_1
    number = LANES // P_SIZE
    for group in range(GROUPS):
        if group:
            first, second = times_of(first, eight), times_of(second, eight)
        values = [first, second]
        for inner in range(number):
            if inner >= 2:
                values.append(
                    tuple(factor * values[-1][i] - values[-2][i] for i in range(2))
                )
            for i in range(2):
                row = group * 2 * LANES + i * LANES + inner * P_SIZE
                u_ref[pl.ds(row, P_SIZE), :] = values[inner][i].astype(bf16)
        yield


def v_groups(lateral, first, end, beam_re, beam_im):
    xs = iota((XW, LANES), 0).astype(f32)
    freq = (iota((XW, LANES), 1) // P_SIZE + KLO).astype(f32) * (omega_step / width_scale)
    away = xs - lateral
    minus = -(away * away)
    inside = (xs >= first) & (xs < end)
    gauss = jnp.where(inside, jnp.exp(minus * freq), 0.0) * (1.0 / math.sqrt(P_SIZE * NF))
    ratio = jnp.exp(minus * ((LANES // P_SIZE) * omega_step / width_scale))
    for group in range(GROUPS):
        lanes = slice(group * LANES, (group + 1) * LANES)
        yield jnp.concatenate(
            [(gauss * beam_re[:, lanes]).astype(bf16), (gauss * beam_im[:, lanes]).astype(bf16)],
            axis=1,
        )
        gauss = gauss * ratio


def contributions(windows, u_ref, ready_ref=None):
    blocks = []
    ready = 0 if ready_ref is None else ready_ref.shape[0]
    later = [
        u_groups(u_ref.at[i - ready], *windows[i][:2]) for i in range(ready, len(windows))
    ]
    if not ready:
        for _ in later.pop(0):
            pass
    for i, window in enumerate(windows):
        following = later.pop(0) if later else iter(())
        held = ready_ref.at[i] if i < ready else u_ref.at[i - ready]
        total = None
        for group, v in enumerate(v_groups(*window[2:])):
            part = dot(v, held[pl.ds(group * 2 * LANES, 2 * LANES), :])
            total = part if total is None else total + part
            next(following, None)
        blocks.append(total)
    return blocks


def u_kernel(rays_ref, out_ref):
    for i in range(out_ref.shape[0]):
        for _ in u_groups(out_ref.at[i], rays_ref[i, :P_SIZE], rays_ref[i, P_SIZE:]):
            pass


def pack_kernel(place_ref, times_ref, amps_ref, second_ref, third_ref, near_ref):
    place = place_ref[0]

    def pack(w, ref):
        ref[0:P_SIZE] = times_ref[w]
        ref[P_SIZE:] = amps_ref[w]

    base = jnp.where(place < GROUP // 2, 0, WIN - place)
    for i in range(HALF):
        pack(jnp.minimum(base + i, WIN - 1), second_ref.at[i])
    pack(jnp.where(place == 1, WIN - 1, 0), third_ref)
    for i in range(GROUP):
        pack(HALF - place + i, near_ref.at[i])


def tails_kernel(slab_ref, foot_ref, lateral_ref, tail_ref, flag_ref):
    slab = slab_ref[0]
    place = slab % GROUP
    first_chip = place < GROUP // 2
    base = jnp.where(first_chip, HALF + 1 + place, 0)
    second = slab + by_place(place, SECOND_STEP)
    third = slab + by_place(place, THIRD_STEP)
    windows = [(slab, HALF - place + i) for i in range(GROUP)]
    windows += [(second, jnp.minimum(base + i, WIN - 1)) for i in range(HALF)]
    windows += [(third, jnp.where(first_chip, WIN - 1, 0))]
    slabs = lateral_ref.shape[2]
    spread = iota((P_SIZE, LANES), 1) % P_SIZE == iota((P_SIZE, LANES), 0)
    sub = iota((8, LANES), 0)
    for i, (centre, w) in enumerate(windows):
        lateral = jnp.where(iota((P_SIZE, slabs), 1) == centre, lateral_ref[w], 0.0)
        lateral = jnp.sum(lateral, axis=1, keepdims=True)
        lateral = jnp.sum(jnp.where(spread, lateral, 0.0), axis=0, keepdims=True)
        foot = jnp.where(iota((2, slabs), 1) == centre, foot_ref[w].astype(f32), 0.0)
        foot = jnp.sum(foot, axis=1, keepdims=True)
        tail_ref[i] = jnp.where(sub == 0, lateral, jnp.where(sub == 1, foot[0:1], foot[1:2]))
    flag_ref[...] = jnp.full(flag_ref.shape, place.astype(f32))


def unpack(rays, tail):
    return rays[:P_SIZE], rays[P_SIZE:], tail[0:1], tail[1:2], tail[2:3]


def near_kernel(
    arrived_ref, spread_ref, cos_ref, sin_ref, rays_ref, tail_ref, ready_ref, near_ref, beam_ref, u_ref,
    *, scale,
):
    own, second, third = slant_stack(
        arrived_ref[...], spread_ref[...], cos_ref[...], sin_ref[...], scale
    )
    for i, beam in enumerate(second + third):
        beam_ref[i : i + 1] = beam
    windows = [unpack(rays_ref[i], tail_ref[i]) + own for i in range(GROUP)]
    for i, block in enumerate(contributions(windows, u_ref, ready_ref)):
        near_ref[i] = block


def far_kernel(
    flag_ref, tail_ref, near_ref, beam_ref, second_ref, third_0_ref, third_1_ref, out_ref, u_ref,
    *, parts,
):
    second, third = (beam_ref[0:1], beam_ref[1:2]), (beam_ref[2:3], beam_ref[3:4])
    windows = [unpack(second_ref[i], tail_ref[GROUP + i]) + second for i in range(HALF)]
    windows += [unpack(third_0_ref[...] + third_1_ref[...], tail_ref[GROUP + HALF]) + third]
    a, b, c, d = contributions(windows, u_ref)
    rows = out_ref.shape[1]
    place = flag_ref[0:1, :]
    is_0, is_2, is_3 = place == 0.0, place == 2.0, place == 3.0
    first = place < GROUP / 2

    def when(condition, block):
        return jnp.where(condition, block, 0.0)

    totals = (
        near_ref[0] + when(first, a + d),
        near_ref[1] + when(first, b) + when(is_3, a),
        near_ref[2] + when(is_0, c) + when(is_3, b) + when(is_2, a),
        near_ref[3] + when(is_3, c) + when(is_2, b) + when(~first, d),
    )
    for t, total in enumerate(totals):
        total = total.T.astype(bf16)
        for i, o in enumerate(parts):
            out_ref[i * GROUP + t] = total[o * rows : (o + 1) * rows]


def total_kernel(parts_ref, out_ref):
    total = parts_ref[0].astype(f32)
    for i in range(1, parts_ref.shape[0]):
        total = total + parts_ref[i].astype(f32)
    out_ref[...] = total


def vmem():
    return pl.BlockSpec(memory_space=pltpu.VMEM)


def smem():
    return pl.BlockSpec(memory_space=pltpu.SMEM)


def call(kernel, out_shape, in_specs, mib=None, scratch=(), flops=0):
    many = isinstance(out_shape, tuple)
    limit = None if mib is None else mib * 1024 * 1024
    return pl.pallas_call(
        kernel,
        out_shape=out_shape,
        in_specs=in_specs,
        out_specs=tuple(vmem() for _ in out_shape) if many else vmem(),
        scratch_shapes=scratch,
        compiler_params=pltpu.CompilerParams(vmem_limit_bytes=limit),
        cost_estimate=pl.CostEstimate(flops=flops, bytes_accessed=1 << 20, transcendentals=0),
    )


def struct(*shape):
    return jax.ShapeDtypeStruct(shape, bf16)


def struct32(*shape):
    return jax.ShapeDtypeStruct(shape, f32)


def shards(traces, centre_ids, midpoint_bins, ray_times, ray_amps, beam_lateral, footprint):
    slab_axes = ("group", "chip", "core")
    my_slab = lax.axis_index(slab_axes)
    slabs = lax.axis_size(slab_axes)
    offsets = lax.axis_size("offset")
    count = traces.shape[1]
    depth = ray_times.shape[4]
    part = depth // offsets
    high, low = dft_tables()
    groups = [(FIRST_SLAB // GROUP + i) % (slabs // GROUP) for i in range(slabs // GROUP)]
    order = [(FIRST_SLAB + i) % slabs for i in range(slabs)]
    routed = call(functools.partial(route_kernel, groups=groups), struct(slabs * ROWS, LANES), [vmem()] * 2 + [pl.BlockSpec(memory_space=pl.ANY)] * 3, None, [
        pltpu.VMEM((count, NT), bf16), pltpu.VMEM((NT, LANES), bf16),
        pltpu.VMEM((NT, LANES), bf16), pltpu.SemaphoreType.DMA((3,)),
    ])(
        centre_ids.reshape(1, count), midpoint_bins, traces[0], jnp.asarray(high), jnp.asarray(low)
    )
    arrived = lax.all_to_all(
        routed.reshape(slabs, ROWS, LANES), slab_axes, split_axis=0, concat_axis=0,
        axis_index_groups=[order], tiled=True,
    ).reshape(slabs * ROWS, LANES)

    place = (my_slab % GROUP).astype(jnp.int32).reshape(1)

    def to_those(steps):
        pairs = [(i + steps[i % GROUP], i) for i in range(slabs) if steps[i % GROUP]]
        return [(i, j) for i, j in pairs if 0 <= i < slabs]

    ray_rows = 2 * P_SIZE
    u_rows = 2 * P_SIZE * NF
    second_rays, third_rays, near_rays = call(
        pack_kernel,
        (
            struct32(HALF, ray_rows, depth), struct32(ray_rows, depth),
            struct32(GROUP, ray_rows, depth),
        ),
        [smem()] + [vmem()] * 2,
        8,
        flops=1 << 28,
    )(place, ray_times[0, 0], ray_amps[0, 0])
    second_rays = lax.ppermute(second_rays, slab_axes, to_those(SECOND_STEP))
    third_0 = lax.ppermute(third_rays, slab_axes, to_those((THIRD_STEP[0], 0, 0, THIRD_STEP[3])))
    third_1 = lax.ppermute(third_rays, slab_axes, to_those((0, THIRD_STEP[1], THIRD_STEP[2], 0)))

    tails, flags = call(
        tails_kernel,
        (struct32(GROUP + HALF + 1, 8, LANES), struct32(8, depth)),
        [smem()] + [vmem()] * 2,
        8,
        flops=1 << 28,
    )(
        my_slab.astype(jnp.int32).reshape(1),
        footprint.transpose(1, 2, 0),
        beam_lateral[0].transpose(1, 2, 0),
    )

    cosine, sine, spread = slant_tables()
    ready = call(u_kernel, struct(READY, u_rows, depth), [vmem()], 8, flops=1 << 28)(near_rays)
    near, beams = call(
        functools.partial(near_kernel, scale=1.0 / math.sqrt(NT * count)),
        (struct32(GROUP, XW, depth), struct32(4, NF * P_SIZE)),
        [vmem()] * 7,
        24,
        [pltpu.VMEM((GROUP - READY, u_rows, depth), bf16)],
    )(
        arrived, jnp.asarray(spread), jnp.asarray(cosine), jnp.asarray(sine), near_rays, tails,
        ready,
    )
    parts = [(FIRST_OFFSET + i) % offsets for i in range(offsets)]
    merged = call(
        functools.partial(far_kernel, parts=parts),
        struct(GROUP * offsets, part, XW),
        [vmem()] * 7,
        24,
        [pltpu.VMEM((HALF + 1, u_rows, depth), bf16)],
    )(flags, tails, near, beams, second_rays, third_0, third_1)
    parts = lax.all_to_all(
        merged, ("offset", "chip", "core"), split_axis=0, concat_axis=0,
        axis_index_groups=[[o * GROUP + t for o in parts for t in range(GROUP)]], tiled=True,
    )
    return call(total_kernel, struct32(part, XW), [vmem()], 4)(parts)


def solution(mesh):
    offsets, slabs = mesh.devices.shape
    shape = (offsets, slabs // GROUP, GROUP // 2, 2)
    chips = Mesh(mesh.devices.reshape(shape), ("offset", "group", "chip", "core"))
    slab = ("group", "chip", "core")
    return jax.shard_map(
        shards,
        mesh=chips,
        in_specs=(
            P("offset", slab, None),
            P("offset", slab, None),
            P("offset", slab),
            P("offset", slab, None, None, None),
            P("offset", slab, None, None, None),
            P("offset", None, None, None),
            P(),
        ),
        out_specs=P("offset", slab),
        check_vma=False,
    )
```
